128 devices in a mesh: gx: 8 (over y, core), gy: 16 (over z, x).
Axes of the slice: x: 4, y: 4, z: 4, core: 2. Of those that a mesh axis runs over, the one named last changes fastest.
Arguments:
- ice_volume: float32 [5, 2048, 4096], P(None, 'gy', 'gx'), may hold values from 0.1 to 1
- ice_area: float32 [5, 2048, 4096], P(None, 'gy', 'gx'), may hold values from 0.15 to 0.2
- velocity: float32 [2, 2048, 4096], P(None, 'gy', 'gx'), may hold values from -3 to 3
- forcing: float32 [2, 2048, 4096], P(None, 'gy', 'gx'), may hold values from -6 to 6
- current: float32 [2, 2048, 4096], P(None, 'gy', 'gx'), may hold values from -3 to 3
- stress: float32 [3, 2048, 4096], P(None, 'gy', 'gx'), may hold values from -3 to 3
- ice_mask: int32 [2048, 4096], P('gy', 'gx'), may hold values from 0 to 1
- block_owner: int32 [128, 256], P('gy', 'gx'), may hold values from -1 to 15, as said below
Outputs:
- stress_out: float32 [3, 2048, 4096], P(None, 'gy', 'gx')
- ice_velocity: float32 [2, 8, 4096, 256], P(None, 'gx', 'gy')
The draws below stay inside these ranges and needn't reach their ends.
Inputs may be any that keep to these rules, and one draw needn't show every extreme that they name: `block_owner`: -1 exactly on the blocks with no ice cell; on every other block the gy index of its owner, which lies in the same gx column; one device's tile hands at most 16 blocks to one owner, and in every draw some tiles hand exactly 16 to every owner.
All inputs are finite; a program needn't handle non-finite values.
Results may differ from the reference program's by a relative error of at most 0.00002.
Values sent between devices are 32-bit elements; how exact they have to be, the bound alone decides.
A program may use at most 192 MiB of HBM per device.

```python
import jax
import jax.numpy as jnp
from jax import lax

NCAT = 5
BLOCK = 16
SUBCYCLES = 4
TLAT = 128
TLON = 512
BPD = 256
CAP = 16
NLAT = 2048
NLON = 4096
N_GX = 8
N_GY = 16


def iced_blocks(key):
    block_rows = NLAT // BLOCK
    block_cols = NLON // BLOCK
    polar_band = TLAT // BLOCK
    tile_cols = TLON // BLOCK
    row_index = jnp.arange(block_rows, dtype=jnp.int32)[:, None]
    col_index = jnp.arange(block_cols, dtype=jnp.int32)[None, :]
    row_offset = jnp.abs(2 * row_index + 1 - block_rows)
    threshold = jnp.maximum(6 * row_offset - 3 * block_rows, block_rows // 2)
    dice_rolls = jax.random.randint(jax.random.fold_in(key, 11), (block_rows, block_cols), 0, 2 * block_rows)
    polar_rows = (row_index < polar_band) | (row_index >= block_rows - polar_band)
    edge_cols = (col_index % tile_cols == 0) | (col_index % tile_cols == tile_cols - 1)
    return (dice_rolls < threshold) | polar_rows | edge_cols


def draw_ice_mask(key, part):
    blocks = iced_blocks(key)
    ice_cells = jnp.repeat(jnp.repeat(blocks, BLOCK, axis=0), BLOCK, axis=1)
    dice_rolls = jax.random.randint(jax.random.fold_in(key, 12), (NLAT, NLON), 0, 10) < 8
    lat_first = jnp.arange(NLAT, dtype=jnp.int32)[:, None] % BLOCK == 0
    lon_first = jnp.arange(NLON, dtype=jnp.int32)[None, :] % BLOCK == 0
    corner_cell = lat_first & lon_first
    return (ice_cells & (dice_rolls | corner_cell)).astype(jnp.int32)


def draw_block_owner(key, part):
    blocks = iced_blocks(key).astype(jnp.int32)
    polar_band = TLAT // BLOCK
    tile_cols = TLON // BLOCK
    per_tile = polar_band * tile_cols
    local_ice = blocks.reshape(N_GY, polar_band, N_GX, tile_cols).transpose(2, 0, 1, 3).reshape(N_GX, N_GY, per_tile)
    rank_order = jnp.cumsum(local_ice, axis=2) - 1
    capacity = per_tile // N_GY
    first_owner = jax.random.randint(jax.random.fold_in(key, 13), (N_GX, N_GY, 1), 0, N_GY)
    owner_map = jnp.where(local_ice > 0, (first_owner + rank_order // capacity) % N_GY, -1)
    owner_map = owner_map.reshape(N_GX, N_GY, polar_band, tile_cols).transpose(1, 2, 0, 3)
    return owner_map.reshape(N_GY * polar_band, N_GX * tile_cols).astype(jnp.int32)


def block_scale(stream_key, shape, cuts, low, largest):
    loudness = 1.0
    for axis_at, parts in cuts:
        draws = jax.random.uniform(jax.random.fold_in(jax.random.fold_in(stream_key, 6), axis_at), (parts,), jnp.float32, low / len(cuts), largest / len(cuts))
        loudness = loudness * jnp.repeat(jnp.exp(draws), shape[axis_at] // parts).reshape((-1,) + (1,) * (len(shape) - 1 - axis_at))
    return loudness


def noise(stream_key, dims, spread, limit, pieces=(), held_as=jnp.bfloat16):
    level = block_scale(stream_key, dims, pieces, -0.22, 0.18) if pieces else 1.0
    result = jax.random.normal(stream_key, dims, jnp.float32) * spread * level
    return jnp.minimum(jnp.maximum(result, -limit), limit).astype(held_as)


def setup_inputs(seed: int = 0) -> dict:
    splits = jax.random.split(jax.random.key(seed), 9)
    ice_volume = jnp.clip(0.1 + 0.9 * jax.random.uniform(splits[0], (NCAT, NLAT, NLON), jnp.float32) ** block_scale(splits[0], (NCAT, NLAT, NLON), ((1, 16), (2, 8)), -0.2, 0.2), 0.1, 1.0)
    ice_area = jnp.clip(0.15 + 0.049999997 * jax.random.uniform(splits[1], (NCAT, NLAT, NLON), jnp.float32) ** block_scale(splits[1], (NCAT, NLAT, NLON), ((1, 16), (2, 8)), -0.2, 0.2), 0.15, 0.2)
    velocity = noise(splits[2], (2, NLAT, NLON), 0.5, 3.0, ((1, 16), (2, 8)), jnp.float32)
    forcing = noise(splits[3], (2, NLAT, NLON), 1.0, 6.0, ((1, 16), (2, 8)), jnp.float32)
    current = noise(splits[4], (2, NLAT, NLON), 0.5, 3.0, ((1, 16), (2, 8)), jnp.float32)
    stress = noise(splits[5], (3, NLAT, NLON), 0.5, 3.0, ((1, 16), (2, 8)), jnp.float32)
    ice_mask = draw_ice_mask(jax.random.fold_in(splits[8], 71), 0)
    block_owner = draw_block_owner(jax.random.fold_in(splits[8], 71), 0)
    return dict(ice_volume=ice_volume, ice_area=ice_area, velocity=velocity, forcing=forcing, current=current, stress=stress, ice_mask=ice_mask, block_owner=block_owner)


STRENGTH_SCALE = 2.0
CONC_DECAY = 20.0
ECC_SQUARED = 4.0
DELTA_FLOOR = 0.1
STRESS_RATE = 0.5
MASS_BASE = 0.5
WATER_DRAG = 0.5
CORIOLIS = 0.3

def shifted(array_in, axis_number, direction):
    axis_number = axis_number % array_in.ndim
    extent = array_in.shape[axis_number]
    padding = jnp.zeros_like(lax.slice_in_dim(array_in, 0, 1, axis=axis_number))
    if direction > 0:
        return jnp.concatenate([lax.slice_in_dim(array_in, 1, extent, axis=axis_number), padding], axis=axis_number)
    return jnp.concatenate([padding, lax.slice_in_dim(array_in, 0, extent - 1, axis=axis_number)], axis=axis_number)

def stress_half(sig_one, sig_two, sig_shear, strain_lon, strain_lat, strain_cross, strength, icemask):
    divergence = strain_lon + strain_lat
    tension = strain_lon - strain_lat
    shearing = 2.0 * strain_cross
    delta = jnp.sqrt(divergence * divergence + (tension * tension + shearing * shearing) / ECC_SQUARED + DELTA_FLOOR * DELTA_FLOOR)
    ratio = strength / delta
    relax_factor = 1.0 + STRESS_RATE
    new_one = (sig_one + STRESS_RATE * (ratio * divergence - strength)) / relax_factor * icemask
    new_two = (sig_two + STRESS_RATE * ratio * tension / ECC_SQUARED) / relax_factor * icemask
    new_shear = (sig_shear + STRESS_RATE * ratio * shearing / (2.0 * ECC_SQUARED)) / relax_factor * icemask
    return (new_one, new_two, new_shear)

def momentum_half(vel_east, vel_north, normal_east, normal_north, sig_shear, east_behind, shear_behind_lon, shear_behind_lat, north_behind, mass, drive_east, drive_north, icemask):
    force_east = normal_east - east_behind + (sig_shear - shear_behind_lat)
    force_north = sig_shear - shear_behind_lon + (normal_north - north_behind)
    denominator = mass + WATER_DRAG
    new_east = (mass * vel_east + force_east + drive_east + CORIOLIS * mass * vel_north) / denominator * icemask
    new_north = (mass * vel_north + force_north + drive_north - CORIOLIS * mass * vel_east) / denominator * icemask
    return (new_east, new_north)

def reference(ice_volume, ice_area, velocity, forcing, current, stress, ice_mask, block_owner):
    icemask = ice_mask.astype(jnp.float32)
    total_volume = lax.optimization_barrier(jnp.sum(ice_volume, axis=0))
    concentration = lax.optimization_barrier(jnp.sum(ice_area, axis=0))
    strength = STRENGTH_SCALE * total_volume * jnp.exp(-CONC_DECAY * (1.0 - concentration))
    mass = MASS_BASE + total_volume
    drive_east = forcing[0] + WATER_DRAG * current[0]
    drive_north = forcing[1] + WATER_DRAG * current[1]
    vel_east = velocity[0] * icemask
    vel_north = velocity[1] * icemask
    sig_one = stress[0] * icemask
    sig_two = stress[1] * icemask
    sig_shear = stress[2] * icemask
    for number in range(SUBCYCLES):
        strain_lon = shifted(vel_east, -1, 1) - vel_east
        strain_lat = shifted(vel_north, -2, 1) - vel_north
        strain_cross = 0.5 * (shifted(vel_east, -2, 1) - vel_east + (shifted(vel_north, -1, 1) - vel_north))
        sig_one, sig_two, sig_shear = stress_half(sig_one, sig_two, sig_shear, strain_lon, strain_lat, strain_cross, strength, icemask)
        normal_east = 0.5 * (sig_one + sig_two)
        normal_north = 0.5 * (sig_one - sig_two)
        vel_east, vel_north = momentum_half(vel_east, vel_north, normal_east, normal_north, sig_shear, shifted(normal_east, -1, -1), shifted(sig_shear, -1, -1), shifted(sig_shear, -2, -1), shifted(normal_north, -2, -1), mass, drive_east, drive_north, icemask)
    stress_out = jnp.stack([sig_one, sig_two, sig_shear])
    block_rows = TLAT // BLOCK
    block_cols = TLON // BLOCK
    final_vel = jnp.stack([vel_east, vel_north])
    vel_blocks = final_vel.reshape(2, N_GY, block_rows, BLOCK, N_GX, block_cols, BLOCK)
    vel_blocks = vel_blocks.transpose(4, 1, 2, 5, 0, 3, 6).reshape(N_GX, N_GY, BPD, 2, BLOCK * BLOCK)
    owners = block_owner.reshape(N_GY, block_rows, N_GX, block_cols).transpose(2, 0, 1, 3).reshape(N_GX, N_GY, BPD)
    onehot = (owners[..., None] == jnp.arange(N_GY, dtype=jnp.int32)).astype(jnp.int32)
    ranks = lax.optimization_barrier(jnp.sum(onehot * (jnp.cumsum(onehot, axis=2) - 1), axis=3)).astype(jnp.int32)
    target = jnp.where(owners >= 0, owners, N_GY).astype(jnp.int32)
    column_idx = jnp.broadcast_to(jnp.arange(N_GX, dtype=jnp.int32)[:, None, None], owners.shape)
    source_idx = jnp.broadcast_to(jnp.arange(N_GY, dtype=jnp.int32)[None, :, None], owners.shape)
    placed = jnp.zeros((N_GX, N_GY, N_GY, CAP, 2, BLOCK * BLOCK), jnp.float32)
    placed = placed.at[column_idx, target, source_idx, ranks].set(vel_blocks, mode='drop')
    ice_velocity = placed.transpose(4, 0, 1, 2, 3, 5).reshape(2, N_GX, N_GY * BPD, BLOCK * BLOCK)
    return (stress_out, ice_velocity)
```

```python
import functools

import jax
import jax.numpy as jnp
from jax import lax
from jax.experimental import pallas as pl
from jax.experimental.pallas import tpu as pltpu
from jax.sharding import PartitionSpec as P

MESH = pl.DeviceIdType.MESH
BLOCK = 16
SUBCYCLES = 4
ROWS, COLS = 128, 512
TOP = 16
HIGH = ROWS + 32
KEEP = 2.0 / 3.0
PEERS = (
    (2, 2), (2, 3), (3, 2), (2, 1), (1, 2), (2, 0), (0, 2), (3, 1),
    (1, 3), (3, 3), (1, 1), (3, 0), (0, 3), (1, 0), (0, 1),
)
U, V, N1, N2, SH, S, B, DE, DN = range(9)


def lanes(n=8):
    return lax.broadcasted_iota(jnp.int32, (n, 128), 1)


def sublanes():
    return lax.broadcasted_iota(jnp.int32, (8, 128), 0)


def prepare(raw, F):
    vol, area, vel, forc, cur, strs, mask = raw

    def rows(i, carry):
        src = pl.ds(pl.multiple_of(i * 8, 8), 8)
        dst = pl.ds(pl.multiple_of(i * 8 + TOP, 8), 8)
        for j in range(4):
            col = pl.ds(j * 128, 128)
            m = mask[src, col].astype(jnp.float32)
            v = [vol[c, src, col] for c in range(5)]
            a = [area[c, src, col] for c in range(5)]
            total = ((v[0] + v[1]) + (v[2] + v[3])) + v[4]
            conc = ((a[0] + a[1]) + (a[2] + a[3])) + a[4]
            strength = 2.0 * total * jnp.exp(-20.0 * (1.0 - conc))
            weight = m / (total + 1.0)
            F[S][j, dst, :] = strength * m * (1.0 / 6.0)
            F[B][j, dst, :] = weight
            F[DE][j, dst, :] = weight * (forc[0, src, col] + 0.5 * cur[0, src, col])
            F[DN][j, dst, :] = weight * (forc[1, src, col] + 0.5 * cur[1, src, col])
            F[U][j, dst, :] = vel[0, src, col] * m
            F[V][j, dst, :] = vel[1, src, col] * m
            half = 0.5 * m
            F[N1][j, dst, :] = half * (strs[0, src, col] + strs[1, src, col])
            F[N2][j, dst, :] = half * (strs[0, src, col] - strs[1, src, col])
            F[SH][j, dst, :] = strs[2, src, col] * m
        return carry

    lax.fori_loop(0, ROWS // 8, rows, 0)


def pack_lon(F, W):
    lane = lanes()

    def rows(i, carry):
        src = pl.ds(pl.multiple_of(i * 8 + TOP, 8), 8)
        out = jnp.zeros((8, 128), jnp.float32)
        for f in range(9):
            x = jnp.where(lane < 64, F[f][0, src, :], F[f][3, src, :])
            x = pltpu.roll(x, 8 * f, 1) if f else x
            here = (lane < 8 * f + 4) & (lane >= 8 * f - 4) if f else (lane < 4) | (lane >= 124)
            out = jnp.where(here, x, out)
        W[pl.ds(pl.multiple_of(i * 8, 8), 8), :] = out
        return carry

    lax.fori_loop(0, ROWS // 8, rows, 0)


def pack_lat(F, send_n, send_s):
    low = sublanes() < 4
    for p in range(5):
        f, g = 2 * p, min(2 * p + 1, 8)
        for j in range(4):
            last = pl.ds(TOP + ROWS - 8, 8)
            first = pl.ds(TOP, 8)
            send_n[p, j] = jnp.where(low, pltpu.roll(F[f][j, last, :], 4, 0), F[g][j, last, :])
            send_s[p, j] = jnp.where(low, F[f][j, first, :], pltpu.roll(F[g][j, first, :], 4, 0))


def unpack_lat(F, recv_s, recv_n, has_s, has_n):
    for p in range(5):
        f, g = 2 * p, 2 * p + 1
        for j in range(4):
            x = recv_s[p, j] * has_s
            y = recv_n[p, j] * has_n
            F[f][j, pl.ds(TOP - 8, 8), :] = pltpu.roll(x, 4, 0)
            F[f][j, pl.ds(TOP + ROWS, 8), :] = y
            if g < 9:
                F[g][j, pl.ds(TOP - 8, 8), :] = x
                F[g][j, pl.ds(TOP + ROWS, 8), :] = pltpu.roll(y, 4, 0)


def unpack_lon(F, WE, WW, has_e, has_w, has_s, has_n):
    ahead = lanes() % 8 < 4

    def tile(r, factor):
        src = pl.ds(r, 8)
        x = jnp.where(ahead, WE[src, :] * (has_e * factor), WW[src, :] * (has_w * factor))
        for f in range(9):
            F[f][4, src, :] = pltpu.roll(x, 128 - 8 * f, 1) if f else x

    def rows(i, carry):
        tile(pl.multiple_of(i * 8 + TOP, 8), 1.0)
        return carry

    lax.fori_loop(0, ROWS // 8, rows, 0)
    tile(TOP - 8, has_s)
    tile(TOP + ROWS, has_n)


def subcycle_rows(F, r, n):
    lane = lanes(n)
    not_last, not_first = lane < 127, lane > 0
    at = lambda f, j, off=0: F[f][j, pl.ds(r + off, n), :]
    u = [at(U, j) for j in range(5)]
    v = [at(V, j) for j in range(5)]
    ru = [pltpu.roll(x, 127, 1) for x in u]
    rv = [pltpu.roll(x, 127, 1) for x in v]
    n1, n2, sh = [], [], []
    for j in range(5):
        k = (j + 1) % 5
        un, vn = at(U, j, 1), at(V, j, 1)
        ue = jnp.where(not_last, ru[j], ru[k])
        ve = jnp.where(not_last, rv[j], rv[k])
        a = ue - u[j]
        b = vn - v[j]
        shear = (un - u[j]) + (ve - v[j])
        div = a + b
        ten = a - b
        q = div * div + 0.25 * (ten * ten + shear * shear) + 0.01
        s = at(S, j)
        t = s * lax.rsqrt(q)
        t4 = 0.25 * t
        g = t * div - s
        h = t4 * ten
        n1.append(KEEP * at(N1, j) + (g + h))
        n2.append(KEEP * at(N2, j) + (g - h))
        sh.append(KEEP * at(SH, j) + t4 * shear)
    for j in range(5):
        F[N1][j, pl.ds(r, n), :] = n1[j]
        F[N2][j, pl.ds(r, n), :] = n2[j]
        F[SH][j, pl.ds(r, n), :] = sh[j]
    r1 = [pltpu.roll(x, 1, 1) for x in n1]
    r3 = [pltpu.roll(x, 1, 1) for x in sh]
    for j in range(5):
        k = (j + 4) % 5
        n1w = jnp.where(not_first, r1[j], r1[k])
        shw = jnp.where(not_first, r3[j], r3[k])
        fx = (n1[j] - n1w) + (sh[j] - at(SH, j, -1))
        fy = (sh[j] - shw) + (n2[j] - at(N2, j, -1))
        w = at(B, j)
        keep = 1.0 - 0.5 * w
        F[U][j, pl.ds(r, n), :] = keep * (u[j] + 0.3 * v[j]) + (w * fx + at(DE, j))
        F[V][j, pl.ds(r, n), :] = keep * (v[j] - 0.3 * u[j]) + (w * fy + at(DN, j))


def subcycles(F):
    def one(_, carry):
        def rows(i, c):
            for t in range(3):
                subcycle_rows(F, pl.multiple_of(TOP - 8 + 16 * (3 * i + t), 8), 16)
            return c

        lax.fori_loop(0, (ROWS + 16) // 48, rows, 0)
        return carry

    lax.fori_loop(0, SUBCYCLES, one, 0)


def placing(own, place):
    owner = jnp.concatenate(
        [jnp.broadcast_to(own[:, c : c + 1], (8, 128)) for c in range(32)], axis=0
    )
    hot = jnp.where(owner == lanes(256), 1.0, 0.0)
    row = lax.broadcasted_iota(jnp.int32, (256, 256), 0)
    col = lax.broadcasted_iota(jnp.int32, (256, 256), 1)
    before = (col % 8) * 32 + col // 8 < (row % 8) * 32 + row // 8
    before = jnp.where(before, 1.0, 0.0).astype(jnp.bfloat16)
    ranks = jnp.dot(before, hot.astype(jnp.bfloat16), preferred_element_type=jnp.float32)
    rank = jnp.sum(hot * ranks, axis=1, keepdims=True)
    slot = owner.astype(jnp.float32) * 16.0 + rank
    slot = jnp.concatenate([slot, slot], axis=1)
    chosen = jnp.where(slot == col.astype(jnp.float32), 1.0, 0.0)
    place[...] = chosen.T.astype(jnp.bfloat16)


def flatten_blocks(F, blocks):
    group = lanes() // 16
    odd = [(group // 2**t) % 2 == 1 for t in range(3)]
    for c in (U, V):
        for j in range(4):
            for h in range(2):
                x = [F[c][j, pl.ds(TOP + 8 * h + r, 8, stride=16), :] for r in range(8)]
                x = [pltpu.roll(y, 16 * r, 1) if r else y for r, y in enumerate(x)]
                for t in range(3):
                    x = [jnp.where(odd[t], x[(m + 2**t) % 8], x[m]) for m in range(8)]
                for b in range(8):
                    y = x[(8 - b) % 8]
                    y = pltpu.roll(y, 128 - 16 * b, 1) if b else y
                    blocks[pl.ds((8 * j + b) * 8, 8), pl.ds((2 * c + h) * 128, 128)] = y


def gather_blocks(place, blocks, send):
    p = place[...]
    for c in range(2):
        x = blocks[:, pl.ds(256 * c, 256)]
        out = None
        for _ in range(3):
            part = x.astype(jnp.bfloat16)
            term = jnp.dot(p, part, preferred_element_type=jnp.float32)
            out = term if out is None else out + term
            x = x - part.astype(jnp.float32)
        send[c] = out


def dynamics(
    vol_ref, area_ref, vel_ref, forc_ref, cur_ref, strs_ref, mask_ref, own_ref,
    stress_out, vel_out,
    vol, area, vel, forc, cur, strs, mask, own,
    f0, f1, f2, f3, f4, f5, f6, f7, f8,
    W, WE, WW, send_n, send_s, recv_s, recv_n,
    place, blocks, send,
    in_sem, halo_send, halo_recv, out_send, out_recv, own_sem,
):
    F = (f0, f1, f2, f3, f4, f5, f6, f7, f8)
    gx, gy = lax.axis_index("gx"), lax.axis_index("gy")
    n_gx, n_gy = lax.axis_size("gx"), lax.axis_size("gy")
    east, west = lax.rem(gx + 1, n_gx), lax.rem(gx + n_gx - 1, n_gx)
    north, south = lax.rem(gy + 1, n_gy), lax.rem(gy + n_gy - 1, n_gy)

    raw = (vol, area, vel, forc, cur, strs, mask, own)
    sources = (vol_ref, area_ref, vel_ref, forc_ref, cur_ref, strs_ref, mask_ref, own_ref)
    loads = []
    for k, (src, dst) in enumerate(zip(sources, raw)):
        copy = pltpu.make_async_copy(src, dst, in_sem.at[k])
        copy.start()
        loads.append(copy)

    barrier = pltpu.get_barrier_semaphore()
    greeted = [(gx, lax.rem(gy + k, n_gy)) for k in range(1, 16)]
    greeted += [(x, y) for x in (east, west) for y in (gy, north, south)]
    for device in greeted:
        pl.semaphore_signal(barrier, inc=1, device_id=device, device_id_type=MESH)

    for f in F:
        for j in range(5):
            f[j, pl.ds(0, 8), :] = jnp.zeros((8, 128), jnp.float32)
            f[j, pl.ds(HIGH - 8, 8), :] = jnp.zeros((8, 128), jnp.float32)
    for copy in loads:
        copy.wait()
    prepare(raw[:7], F)
    pack_lat(F, send_n, send_s)
    pack_lon(F, W)
    pl.semaphore_wait(barrier, len(greeted))

    first, last = W.at[pl.ds(0, 8), :], W.at[pl.ds(ROWS - 8, 8), :]
    above, below, same = pl.ds(TOP + ROWS, 8), pl.ds(TOP - 8, 8), pl.ds(TOP, ROWS)
    halos = (
        (send_n, recv_s, (gx, north)),
        (send_s, recv_n, (gx, south)),
        (W, WW.at[same, :], (east, gy)),
        (W, WE.at[same, :], (west, gy)),
        (first, WW.at[above, :], (east, south)),
        (first, WE.at[above, :], (west, south)),
        (last, WW.at[below, :], (east, north)),
        (last, WE.at[below, :], (west, north)),
    )
    copies = []
    for k, (src, dst, device) in enumerate(halos):
        copy = pltpu.make_async_remote_copy(
            src_ref=src,
            dst_ref=dst,
            send_sem=halo_send.at[k],
            recv_sem=halo_recv.at[k],
            device_id=device,
            device_id_type=MESH,
        )
        copy.start()
        copies.append(copy)

    placing(own, place)

    for copy in copies:
        copy.wait_recv()
    one, zero = jnp.float32(1.0), jnp.float32(0.0)
    has_e, has_w = jnp.where(gx < n_gx - 1, one, zero), jnp.where(gx > 0, one, zero)
    has_n, has_s = jnp.where(gy < n_gy - 1, one, zero), jnp.where(gy > 0, one, zero)
    unpack_lat(F, recv_s, recv_n, has_s, has_n)
    unpack_lon(F, WE, WW, has_e, has_w, has_s, has_n)

    subcycles(F)
    flatten_blocks(F, blocks)
    gather_blocks(place, blocks, send)

    z, x = gy // 4, lax.rem(gy, 4)
    mine = pl.ds(pl.multiple_of(gy * 16, 16), 16)
    for k, (dz, dx) in enumerate(PEERS):
        to = lax.rem(z + dz, 4) * 4 + lax.rem(x + dx, 4)
        copy = pltpu.make_async_remote_copy(
            src_ref=send.at[:, pl.ds(pl.multiple_of(to * 16, 16), 16), :],
            dst_ref=vel_out.at[:, mine, :],
            send_sem=out_send.at[k],
            recv_sem=out_recv.at[k],
            device_id=(gx, to),
            device_id_type=MESH,
        )
        copy.start()
        copies.append(copy)
    local = pltpu.make_async_copy(send.at[:, mine, :], vel_out.at[:, mine, :], own_sem.at[0])
    local.start()

    def rows(i, carry):
        src = pl.ds(pl.multiple_of(i * 8 + TOP, 8), 8)
        dst = pl.ds(pl.multiple_of(i * 8, 8), 8)
        for j in range(4):
            col = pl.ds(j * 128, 128)
            stress_out[0, dst, col] = F[N1][j, src, :] + F[N2][j, src, :]
            stress_out[1, dst, col] = F[N1][j, src, :] - F[N2][j, src, :]
            stress_out[2, dst, col] = F[SH][j, src, :]
        return carry

    lax.fori_loop(0, ROWS // 8, rows, 0)

    for copy in copies:
        copy.wait_send()
    for copy in copies[len(halos) :]:
        copy.wait_recv()
    local.wait()


def write_out(stress, vel, stress_out, vel_out, sem):
    copies = [
        pltpu.make_async_copy(stress, stress_out, sem.at[0]),
        pltpu.make_async_copy(vel, vel_out, sem.at[1]),
    ]
    for copy in copies:
        copy.start()
    for copy in copies:
        copy.wait()


def per_device(ice_volume, ice_area, velocity, forcing, current, stress, ice_mask, block_owner):
    f32, dma, vmem = jnp.float32, pltpu.SemaphoreType.DMA, pltpu.VMEM
    args = (ice_volume, ice_area, velocity, forcing, current, stress, ice_mask, block_owner)
    args = [pltpu.with_memory_space_constraint(a, pltpu.HBM) for a in args]
    stress_shape, vel_shape = (3, ROWS, COLS), (2, 256, 256)
    scratch = [vmem(a.shape, a.dtype) for a in args]
    scratch += [vmem((5, HIGH, 128), f32)] * 9
    scratch += [vmem((ROWS, 128), f32), vmem((HIGH, 128), f32), vmem((HIGH, 128), f32)]
    scratch += [vmem((5, 4, 8, 128), f32)] * 4
    scratch += [vmem((256, 256), jnp.bfloat16), vmem((256, 512), f32), vmem(vel_shape, f32)]
    scratch += [dma((8,)), dma((8,)), dma((8,)), dma((15,)), dma((15,)), dma((1,))]
    held_stress, held_vel = pl.pallas_call(
        dynamics,
        out_shape=(vmem(stress_shape, f32), vmem(vel_shape, f32)),
        in_specs=[pl.BlockSpec(memory_space=pltpu.HBM)] * 8,
        out_specs=(pl.BlockSpec(memory_space=vmem),) * 2,
        scratch_shapes=scratch,
        compiler_params=pltpu.CompilerParams(
            collective_id=0, has_side_effects=True, vmem_limit_bytes=48 * 2**20
        ),
    )(*args)
    held_stress = pltpu.with_memory_space_constraint(held_stress, vmem)
    held_vel = pltpu.with_memory_space_constraint(held_vel, vmem)
    stress_out, vel_out = pl.pallas_call(
        write_out,
        out_shape=(
            jax.ShapeDtypeStruct(stress_shape, f32),
            jax.ShapeDtypeStruct(vel_shape, f32),
        ),
        in_specs=[pl.BlockSpec(memory_space=vmem)] * 2,
        out_specs=(pl.BlockSpec(memory_space=pl.ANY),) * 2,
        scratch_shapes=[dma((2,))],
    )(held_stress, held_vel)
    return (stress_out, vel_out[:, None])


def solution(mesh):
    tile = P(None, "gy", "gx")
    in_specs = (tile,) * 6 + (P("gy", "gx"),) * 2
    out_specs = (tile, P(None, "gx", "gy", None))
    return jax.shard_map(
        per_device, mesh=mesh, in_specs=in_specs, out_specs=out_specs, check_vma=False
    )
```

```python
import functools

import jax
import jax.numpy as jnp
from jax import lax
from jax.experimental import pallas as pl
from jax.experimental.pallas import tpu as pltpu
from jax.sharding import PartitionSpec as P

MESH = pl.DeviceIdType.MESH
BLOCK = 16
SUBCYCLES = 4
ROWS, COLS = 128, 512
TOP = 16
HIGH = ROWS + 32
KEEP = 2.0 / 3.0
PEERS = (
    (2, 2), (2, 3), (3, 2), (2, 1), (1, 2), (2, 0), (0, 2), (3, 1),
    (1, 3), (3, 3), (1, 1), (3, 0), (0, 3), (1, 0), (0, 1),
)
U, V, N1, N2, SH, S, B, DE, DN = range(9)


def lanes(n=8):
    return lax.broadcasted_iota(jnp.int32, (n, 128), 1)


def sublanes():
    return lax.broadcasted_iota(jnp.int32, (8, 128), 0)


def prepare(raw, F, first, count, step, n, tiles):
    held, mask = raw
    vol, area, vel = held.at[0:5], held.at[5:10], held.at[10:12]
    forc, cur, strs = held.at[12:14], held.at[14:16], held.at[16:19]

    def rows(i, carry):
        row = first + step * i
        src = pl.ds(pl.multiple_of(row, 8), n)
        dst = pl.ds(pl.multiple_of(row + TOP, 8), n)
        for j in tiles:
            col = pl.ds(j * 128, 128)
            m = mask[src, col].astype(jnp.float32)
            v = [vol[c, src, col] for c in range(5)]
            a = [area[c, src, col] for c in range(5)]
            total = ((v[0] + v[1]) + (v[2] + v[3])) + v[4]
            conc = ((a[0] + a[1]) + (a[2] + a[3])) + a[4]
            strength = 2.0 * total * jnp.exp(-20.0 * (1.0 - conc))
            weight = m / (total + 1.0)
            F[S][j, dst, :] = strength * m * (1.0 / 6.0)
            F[B][j, dst, :] = weight
            F[DE][j, dst, :] = weight * (forc[0, src, col] + 0.5 * cur[0, src, col])
            F[DN][j, dst, :] = weight * (forc[1, src, col] + 0.5 * cur[1, src, col])
            F[U][j, dst, :] = vel[0, src, col] * m
            F[V][j, dst, :] = vel[1, src, col] * m
            half = 0.5 * m
            F[N1][j, dst, :] = half * (strs[0, src, col] + strs[1, src, col])
            F[N2][j, dst, :] = half * (strs[0, src, col] - strs[1, src, col])
            F[SH][j, dst, :] = strs[2, src, col] * m
        return carry

    lax.fori_loop(0, count, rows, 0, unroll=count == 2 and n == 8)


def pack_lon(F, W):
    n = 64
    lane = lanes(n)

    def rows(i, carry):
        src = pl.ds(pl.multiple_of(i * n + TOP, 8), n)
        out = jnp.zeros((n, 128), jnp.float32)
        for f in range(9):
            x = jnp.where(lane < 64, F[f][0, src, :], F[f][3, src, :])
            x = pltpu.roll(x, 8 * f, 1) if f else x
            here = (lane < 8 * f + 4) & (lane >= 8 * f - 4) if f else (lane < 4) | (lane >= 124)
            out = jnp.where(here, x, out)
        W[pl.ds(pl.multiple_of(i * n, 8), n), :] = out
        return carry

    lax.fori_loop(0, ROWS // n, rows, 0)


def pack_lat(F, send_n, send_s):
    low = sublanes() < 4
    for p in range(5):
        f, g = 2 * p, min(2 * p + 1, 8)
        for j in range(4):
            last = pl.ds(TOP + ROWS - 8, 8)
            first = pl.ds(TOP, 8)
            send_n[p, j] = jnp.where(low, pltpu.roll(F[f][j, last, :], 4, 0), F[g][j, last, :])
            send_s[p, j] = jnp.where(low, F[f][j, first, :], pltpu.roll(F[g][j, first, :], 4, 0))


def unpack_lat(F, recv_s, recv_n):
    for p in range(5):
        f, g = 2 * p, 2 * p + 1
        for j in range(4):
            x = recv_s[p, j]
            y = recv_n[p, j]
            F[f][j, pl.ds(TOP - 8, 8), :] = pltpu.roll(x, 4, 0)
            F[f][j, pl.ds(TOP + ROWS, 8), :] = y
            if g < 9:
                F[g][j, pl.ds(TOP - 8, 8), :] = x
                F[g][j, pl.ds(TOP + ROWS, 8), :] = pltpu.roll(y, 4, 0)


def unpack_lon(F, WE, WW):
    n = 48
    ahead = lanes(n) % 8 < 4

    def rows(i, carry):
        src = pl.ds(pl.multiple_of(i * n + TOP - 8, 8), n)
        x = jnp.where(ahead, WE[src, :], WW[src, :])
        for f in range(9):
            F[f][4, src, :] = pltpu.roll(x, 128 - 8 * f, 1) if f else x
        return carry

    lax.fori_loop(0, (ROWS + 16) // n, rows, 0)


def subcycle_rows(F, r, n):
    lane = lanes(n)
    not_last, not_first = lane < 127, lane > 0
    at = lambda f, j, off=0: F[f][j, pl.ds(r + off, n), :]
    u = [at(U, j) for j in range(5)]
    v = [at(V, j) for j in range(5)]
    ru = [pltpu.roll(x, 127, 1) for x in u]
    rv = [pltpu.roll(x, 127, 1) for x in v]
    n1, n2, sh = [], [], []
    for j in range(5):
        k = (j + 1) % 5
        un, vn = at(U, j, 1), at(V, j, 1)
        ue = jnp.where(not_last, ru[j], ru[k])
        ve = jnp.where(not_last, rv[j], rv[k])
        a = ue - u[j]
        b = vn - v[j]
        shear = (un - u[j]) + (ve - v[j])
        div = a + b
        ten = a - b
        q = div * div + 0.25 * (ten * ten + shear * shear) + 0.01
        s = at(S, j)
        t = s * lax.rsqrt(q)
        t4 = 0.25 * t
        g = t * div - s
        h = t4 * ten
        n1.append(KEEP * at(N1, j) + (g + h))
        n2.append(KEEP * at(N2, j) + (g - h))
        sh.append(KEEP * at(SH, j) + t4 * shear)
    for j in range(5):
        F[N1][j, pl.ds(r, n), :] = n1[j]
        F[N2][j, pl.ds(r, n), :] = n2[j]
        F[SH][j, pl.ds(r, n), :] = sh[j]
    r1 = [pltpu.roll(x, 1, 1) for x in n1]
    r3 = [pltpu.roll(x, 1, 1) for x in sh]
    for j in range(5):
        k = (j + 4) % 5
        n1w = jnp.where(not_first, r1[j], r1[k])
        shw = jnp.where(not_first, r3[j], r3[k])
        fx = (n1[j] - n1w) + (sh[j] - at(SH, j, -1))
        fy = (sh[j] - shw) + (n2[j] - at(N2, j, -1))
        w = at(B, j)
        keep = 1.0 - 0.5 * w
        F[U][j, pl.ds(r, n), :] = keep * (u[j] + 0.3 * v[j]) + (w * fx + at(DE, j))
        F[V][j, pl.ds(r, n), :] = keep * (v[j] - 0.3 * u[j]) + (w * fy + at(DN, j))


def subcycles(F):
    def one(_, carry):
        def rows(i, c):
            for t in range(3):
                subcycle_rows(F, pl.multiple_of(TOP - 8 + 16 * (3 * i + t), 8), 16)
            return c

        lax.fori_loop(0, (ROWS + 16) // 48, rows, 0)
        return carry

    lax.fori_loop(0, SUBCYCLES, one, 0)


def placing(own, place):
    owner = jnp.concatenate(
        [jnp.broadcast_to(own[:, c : c + 1], (8, 128)) for c in range(32)], axis=0
    )
    hot = jnp.where(owner == lanes(256), 1.0, 0.0)
    row = lax.broadcasted_iota(jnp.int32, (256, 256), 0)
    col = lax.broadcasted_iota(jnp.int32, (256, 256), 1)
    before = (col % 8) * 32 + col // 8 < (row % 8) * 32 + row // 8
    before = jnp.where(before, 1.0, 0.0).astype(jnp.bfloat16)
    ranks = jnp.dot(before, hot.astype(jnp.bfloat16), preferred_element_type=jnp.float32)
    rank = jnp.sum(hot * ranks, axis=1, keepdims=True)
    slot = owner.astype(jnp.float32) * 16.0 + rank
    slot = jnp.concatenate([slot, slot], axis=1)
    chosen = jnp.where(slot == col.astype(jnp.float32), 1.0, 0.0)
    place[...] = chosen.T.astype(jnp.bfloat16)


def flatten_blocks(F, blocks):
    group = lanes() // 16
    odd = [(group // 2**t) % 2 == 1 for t in range(3)]
    for c in (U, V):
        for j in range(4):
            for h in range(2):
                x = [F[c][j, pl.ds(TOP + 8 * h + r, 8, stride=16), :] for r in range(8)]
                x = [pltpu.roll(y, 16 * r, 1) if r else y for r, y in enumerate(x)]
                for t in range(3):
                    x = [jnp.where(odd[t], x[(m + 2**t) % 8], x[m]) for m in range(8)]
                for b in range(8):
                    y = x[(8 - b) % 8]
                    y = pltpu.roll(y, 128 - 16 * b, 1) if b else y
                    blocks[pl.ds((8 * j + b) * 8, 8), pl.ds((2 * c + h) * 128, 128)] = y


def gather_blocks(place, blocks, send):
    p = place[...]
    for c in range(2):
        x = blocks[:, pl.ds(256 * c, 256)]
        out = None
        for _ in range(3):
            part = x.astype(jnp.bfloat16)
            term = jnp.dot(p, part, preferred_element_type=jnp.float32)
            out = term if out is None else out + term
            x = x - part.astype(jnp.float32)
        send[c] = out


def dynamics(
    vol_ref, area_ref, vel_ref, forc_ref, cur_ref, strs_ref, mask_ref, own_ref,
    stress_out, vel_out,
    held, mask, own,
    f0, f1, f2, f3, f4, f5, f6, f7, f8,
    W, WE, WW, send_n, send_s, recv_s, recv_n,
    place, blocks, send,
    in_sem, halo_send, halo_recv, out_sem,
):
    F = (f0, f1, f2, f3, f4, f5, f6, f7, f8)
    gx, gy = lax.axis_index("gx"), lax.axis_index("gy")
    n_gx, n_gy = lax.axis_size("gx"), lax.axis_size("gy")
    east, west = lax.rem(gx + 1, n_gx), lax.rem(gx + n_gx - 1, n_gx)
    north, south = lax.rem(gy + 1, n_gy), lax.rem(gy + n_gy - 1, n_gy)

    has_e, has_w, has_n, has_s = gx < n_gx - 1, gx > 0, gy < n_gy - 1, gy > 0

    barrier = pltpu.get_barrier_semaphore()
    around = (
        (has_e, (east, gy)),
        (has_w, (west, gy)),
        (has_e & has_n, (east, north)),
        (has_e & has_s, (east, south)),
        (has_w & has_n, (west, north)),
        (has_w & has_s, (west, south)),
    )
    for there, device in around:

        @pl.when(there)
        def _(device=device):
            pl.semaphore_signal(barrier, inc=1, device_id=device, device_id_type=MESH)

    for k in range(1, 16):
        pl.semaphore_signal(
            barrier, inc=1, device_id=(gx, lax.rem(gy + k, n_gy)), device_id_type=MESH
        )
    one, zero = jnp.int32(1), jnp.int32(0)
    count = lambda there: jnp.where(there, one, zero)
    greeted = 15 + (count(has_e) + count(has_w)) * (1 + count(has_n) + count(has_s))

    mask_load = pltpu.make_async_copy(mask_ref, mask, in_sem.at[5])
    own_load = pltpu.make_async_copy(own_ref, own, in_sem.at[6])
    mask_load.start()
    every, inner = pl.ds(0, COLS), pl.ds(8, ROWS - 16)
    parts = (
        (pl.ds(0, 8), every),
        (pl.ds(ROWS - 8, 8), every),
        (inner, pl.ds(0, 128)),
        (inner, pl.ds(COLS - 128, 128)),
        (inner, pl.ds(128, COLS - 256)),
    )
    sources = (vol_ref, area_ref, vel_ref, forc_ref, cur_ref, strs_ref)
    loads = []
    for k, (r, c) in enumerate(parts):
        start = 0
        for src in sources:
            dst = held.at[pl.ds(start, src.shape[0]), r, c]
            pltpu.make_async_copy(src.at[:, r, c], dst, in_sem.at[k]).start()
            start += src.shape[0]
        loads.append(pltpu.make_async_copy(held.at[:, r, c], held.at[:, r, c], in_sem.at[k]))
    own_load.start()

    for f in F:
        for j in range(5):
            f[j, pl.ds(0, 8), :] = jnp.zeros((8, 128), jnp.float32)
            f[j, pl.ds(HIGH - 8, 8), :] = jnp.zeros((8, 128), jnp.float32)
    above, below, same = pl.ds(TOP + ROWS, 8), pl.ds(TOP - 8, 8), pl.ds(TOP, ROWS)
    for there, buf in ((has_s, recv_s), (has_n, recv_n)):

        @pl.when(jnp.logical_not(there))
        def _(buf=buf):
            buf[...] = jnp.zeros(buf.shape, jnp.float32)

    for there, buf in ((has_e, WE), (has_w, WW)):
        for beside, at in ((has_n, above), (has_s, below), (there, same)):

            @pl.when(jnp.logical_not(there & beside))
            def _(buf=buf, at=at):
                buf[at, :] = jnp.zeros((at.size, 128), jnp.float32)

    first, last = W.at[pl.ds(0, 8), :], W.at[pl.ds(ROWS - 8, 8), :]
    halos = (
        (send_n, recv_s, (gx, north), has_n, has_s),
        (send_s, recv_n, (gx, south), has_s, has_n),
        (W, WW.at[same, :], (east, gy), has_e, has_w),
        (W, WE.at[same, :], (west, gy), has_w, has_e),
        (first, WW.at[above, :], (east, south), has_e & has_s, has_w & has_n),
        (first, WE.at[above, :], (west, south), has_w & has_s, has_e & has_n),
        (last, WW.at[below, :], (east, north), has_e & has_n, has_w & has_s),
        (last, WE.at[below, :], (west, north), has_w & has_n, has_e & has_s),
    )

    def halo(k):
        src, dst, device, _, _ = halos[k]
        return pltpu.make_async_remote_copy(
            src_ref=src,
            dst_ref=dst,
            send_sem=halo_send.at[k],
            recv_sem=halo_recv.at[k],
            device_id=device,
            device_id_type=MESH,
        )

    def start_halo(k):
        @pl.when(halos[k][3])
        def _():
            halo(k).start()

    mask_load.wait()
    loads[0].wait()
    loads[1].wait()
    prepare((held, mask), F, 0, 2, ROWS - 8, 8, range(4))
    pack_lat(F, send_n, send_s)
    pl.semaphore_wait(barrier, greeted)
    for k in (0, 1):
        start_halo(k)

    loads[2].wait()
    loads[3].wait()
    prepare((held, mask), F, 8, 2, 56, 56, (0, 3))
    pack_lon(F, W)
    for k in range(2, 8):
        start_halo(k)

    loads[4].wait()
    prepare((held, mask), F, 8, 2, 56, 56, (1, 2))
    own_load.wait()
    placing(own, place)

    for k in range(8):

        @pl.when(halos[k][4])
        def _(k=k):
            halo(k).wait_recv()

    unpack_lat(F, recv_s, recv_n)
    unpack_lon(F, WE, WW)

    subcycles(F)
    flatten_blocks(F, blocks)
    gather_blocks(place, blocks, send)

    z, x = gy // 4, lax.rem(gy, 4)
    mine = pl.ds(pl.multiple_of(gy * 16, 16), 16)
    for dz, dx in PEERS:
        to = lax.rem(z + dz, 4) * 4 + lax.rem(x + dx, 4)
        copy = pltpu.make_async_remote_copy(
            src_ref=send.at[:, pl.ds(pl.multiple_of(to * 16, 16), 16), :],
            dst_ref=vel_out.at[:, mine, :],
            send_sem=out_sem.at[0],
            recv_sem=out_sem.at[1],
            device_id=(gx, to),
            device_id_type=MESH,
        )
        copy.start()
    local = pltpu.make_async_copy(send.at[:, mine, :], vel_out.at[:, mine, :], out_sem.at[2])
    local.start()

    def rows(i, carry):
        src = pl.ds(pl.multiple_of(i * 16 + TOP, 8), 16)
        dst = pl.ds(pl.multiple_of(i * 16, 8), 16)
        for j in range(4):
            col = pl.ds(j * 128, 128)
            stress_out[0, dst, col] = F[N1][j, src, :] + F[N2][j, src, :]
            stress_out[1, dst, col] = F[N1][j, src, :] - F[N2][j, src, :]
            stress_out[2, dst, col] = F[SH][j, src, :]
        return carry

    lax.fori_loop(0, ROWS // 16, rows, 0)

    for k in range(8):

        @pl.when(halos[k][3])
        def _(k=k):
            halo(k).wait_send()

    others = pl.ds(0, 240)
    for k in range(2):
        pltpu.make_async_copy(send.at[:, others, :], vel_out.at[:, others, :], out_sem.at[k]).wait()
    local.wait()


def write_out(stress, vel, stress_out, vel_out, sem):
    copies = [
        pltpu.make_async_copy(stress, stress_out, sem.at[0]),
        pltpu.make_async_copy(vel, vel_out, sem.at[1]),
    ]
    for copy in copies:
        copy.start()
    for copy in copies:
        copy.wait()


def per_device(ice_volume, ice_area, velocity, forcing, current, stress, ice_mask, block_owner):
    f32, dma, vmem = jnp.float32, pltpu.SemaphoreType.DMA, pltpu.VMEM
    args = (ice_volume, ice_area, velocity, forcing, current, stress, ice_mask, block_owner)
    args = [pltpu.with_memory_space_constraint(a, pltpu.HBM) for a in args]
    stress_shape, vel_shape = (3, ROWS, COLS), (2, 256, 256)
    scratch = [vmem((19, ROWS, COLS), f32)] + [vmem(a.shape, a.dtype) for a in args[6:]]
    scratch += [vmem((5, HIGH, 128), f32)] * 9
    scratch += [vmem((ROWS, 128), f32), vmem((HIGH, 128), f32), vmem((HIGH, 128), f32)]
    scratch += [vmem((5, 4, 8, 128), f32)] * 4
    scratch += [vmem((256, 256), jnp.bfloat16), vmem((256, 512), f32), vmem(vel_shape, f32)]
    scratch += [dma((7,)), dma((8,)), dma((8,)), dma((3,))]
    held_stress, held_vel = pl.pallas_call(
        dynamics,
        out_shape=(vmem(stress_shape, f32), vmem(vel_shape, f32)),
        in_specs=[pl.BlockSpec(memory_space=pltpu.HBM)] * 8,
        out_specs=(pl.BlockSpec(memory_space=vmem),) * 2,
        scratch_shapes=scratch,
        compiler_params=pltpu.CompilerParams(
            collective_id=0, has_side_effects=True, vmem_limit_bytes=48 * 2**20
        ),
    )(*args)
    held_stress = pltpu.with_memory_space_constraint(held_stress, vmem)
    held_vel = pltpu.with_memory_space_constraint(held_vel, vmem)
    stress_out, vel_out = pl.pallas_call(
        write_out,
        out_shape=(
            jax.ShapeDtypeStruct(stress_shape, f32),
            jax.ShapeDtypeStruct(vel_shape, f32),
        ),
        in_specs=[pl.BlockSpec(memory_space=vmem)] * 2,
        out_specs=(pl.BlockSpec(memory_space=pl.ANY),) * 2,
        scratch_shapes=[dma((2,))],
    )(held_stress, held_vel)
    return (stress_out, vel_out[:, None])


def solution(mesh):
    tile = P(None, "gy", "gx")
    in_specs = (tile,) * 6 + (P("gy", "gx"),) * 2
    out_specs = (tile, P(None, "gx", "gy", None))
    return jax.shard_map(
        per_device, mesh=mesh, in_specs=in_specs, out_specs=out_specs, check_vma=False
    )
```

```python
import functools

import jax
import jax.numpy as jnp
from jax import lax
from jax.experimental import pallas as pl
from jax.experimental.pallas import tpu as pltpu
from jax.sharding import PartitionSpec as P

MESH = pl.DeviceIdType.MESH
BLOCK = 16
SUBCYCLES = 4
ROWS, COLS = 128, 512
TOP = 16
HIGH = ROWS + 32
KEEP = 2.0 / 3.0
PEERS = (
    (2, 2), (2, 3), (3, 2), (2, 1), (1, 2), (2, 0), (0, 2), (3, 1),
    (1, 3), (3, 3), (1, 1), (3, 0), (0, 3), (1, 0), (0, 1),
)
U, V, N1, N2, SH, S, B, DE, DN = range(9)


def lanes(n=8):
    return lax.broadcasted_iota(jnp.int32, (n, 128), 1)


def sublanes():
    return lax.broadcasted_iota(jnp.int32, (8, 128), 0)


def prepare(raw, F, first, count, step, n, tiles):
    held, mask = raw
    vol, area, vel = held.at[0:5], held.at[5:10], held.at[10:12]
    forc, cur, strs = held.at[12:14], held.at[14:16], held.at[16:19]

    def rows(i, carry):
        row = first + step * i
        src = pl.ds(pl.multiple_of(row, 8), n)
        dst = pl.ds(pl.multiple_of(row + TOP, 8), n)
        for j in tiles:
            col = pl.ds(j * 128, 128)
            m = mask[src, col].astype(jnp.float32)
            v = [vol[c, src, col] for c in range(5)]
            a = [area[c, src, col] for c in range(5)]
            total = ((v[0] + v[1]) + (v[2] + v[3])) + v[4]
            conc = ((a[0] + a[1]) + (a[2] + a[3])) + a[4]
            strength = 2.0 * total * jnp.exp(-20.0 * (1.0 - conc))
            weight = m / (total + 1.0)
            F[S][j, dst, :] = strength * m * (1.0 / 3.0)
            F[B][j, dst, :] = 0.5 * weight
            F[DE][j, dst, :] = weight * (forc[0, src, col] + 0.5 * cur[0, src, col])
            F[DN][j, dst, :] = weight * (forc[1, src, col] + 0.5 * cur[1, src, col])
            F[U][j, dst, :] = vel[0, src, col] * m
            F[V][j, dst, :] = vel[1, src, col] * m
            F[N1][j, dst, :] = m * (strs[0, src, col] + strs[1, src, col])
            F[N2][j, dst, :] = m * (strs[0, src, col] - strs[1, src, col])
            F[SH][j, dst, :] = (m + m) * strs[2, src, col]
        return carry

    lax.fori_loop(0, count, rows, 0, unroll=count == 2 and n == 8)


def pack_lon(F, W):
    n = 64
    lane = lanes(n)

    def rows(i, carry):
        src = pl.ds(pl.multiple_of(i * n + TOP, 8), n)
        out = jnp.zeros((n, 128), jnp.float32)
        for f in range(9):
            x = jnp.where(lane < 64, F[f][0, src, :], F[f][3, src, :])
            x = pltpu.roll(x, 8 * f, 1) if f else x
            here = (lane < 8 * f + 4) & (lane >= 8 * f - 4) if f else (lane < 4) | (lane >= 124)
            out = jnp.where(here, x, out)
        W[pl.ds(pl.multiple_of(i * n, 8), n), :] = out
        return carry

    lax.fori_loop(0, ROWS // n, rows, 0)


def pack_lat(F, send_n, send_s):
    low = sublanes() < 4
    for p in range(5):
        f, g = 2 * p, min(2 * p + 1, 8)
        for j in range(4):
            last = pl.ds(TOP + ROWS - 8, 8)
            first = pl.ds(TOP, 8)
            send_n[p, j] = jnp.where(low, pltpu.roll(F[f][j, last, :], 4, 0), F[g][j, last, :])
            send_s[p, j] = jnp.where(low, F[f][j, first, :], pltpu.roll(F[g][j, first, :], 4, 0))


def copy_edges(F, T, G):
    for f in range(9):
        for j in range(4):
            T[f][j, pl.ds(16, 8), :] = F[f][j, pl.ds(TOP, 8), :]
            T[f][j, pl.ds(24, 8), :] = F[f][j, pl.ds(TOP + ROWS - 8, 8), :]
    n = 64

    def rows(i, carry):
        at = pl.ds(pl.multiple_of(i * n + TOP, 8), n)
        for f in range(9):
            G[f][0, at, :] = edge_columns(F[f][0, at, :], F[f][3, at, :])
        return carry

    lax.fori_loop(0, ROWS // n, rows, 0)


def edge_columns(first, last):
    lane = lanes(first.shape[0])
    own = jnp.where(lane < 8, first, 0.0)
    return jnp.where((lane >= 56) & (lane < 64), pltpu.roll(last, 64, 1), own)


def unpack_lat(T, G, recv_s, recv_n):
    behind, ahead = pl.ds(8, 8), pl.ds(32, 8)
    for p in range(5):
        f, g = 2 * p, 2 * p + 1
        for j in range(4):
            x = recv_s[p, j]
            y = recv_n[p, j]
            T[f][j, behind, :] = pltpu.roll(x, 4, 0)
            T[f][j, ahead, :] = y
            if g < 9:
                T[g][j, behind, :] = x
                T[g][j, ahead, :] = pltpu.roll(y, 4, 0)
    for f in range(9):
        G[f][0, pl.ds(TOP - 8, 8), :] = edge_columns(T[f][0, behind, :], T[f][3, behind, :])
        G[f][0, pl.ds(TOP + ROWS, 8), :] = edge_columns(T[f][0, ahead, :], T[f][3, ahead, :])


def unpack_lon(G, WE, WW):
    n = 48
    lane = lanes(n)
    ahead = lane % 8 < 4
    halo = (lane >= 124) | ((lane >= 64) & (lane < 68))

    def rows(i, carry):
        src = pl.ds(pl.multiple_of(i * n + TOP - 8, 8), n)
        x = jnp.where(ahead, pltpu.roll(WE[src, :], 64, 1), WW[src, :])
        for f in range(9):
            y = pltpu.roll(x, 128 - 8 * f, 1) if f else x
            G[f][0, src, :] = jnp.where(halo, y, G[f][0, src, :])
        return carry

    lax.fori_loop(0, (ROWS + 16) // n, rows, 0)


def subcycle_rows(F, r, n):
    tiles = F[0].shape[0]
    lane = lanes(n)
    not_last, not_first = lane < 127, lane > 0
    at = lambda f, j, off=0: F[f][j, pl.ds(r + off, n), :]

    def beside(x, step):
        turned = [pltpu.roll(y, 127 if step > 0 else 1, 1) for y in x]
        if tiles == 1:
            return turned
        inside = not_last if step > 0 else not_first
        return [jnp.where(inside, turned[j], turned[(j + step) % tiles]) for j in range(tiles)]

    u = [at(U, j) for j in range(tiles)]
    v = [at(V, j) for j in range(tiles)]
    ue, ve = beside(u, 1), beside(v, 1)
    n1, n2, sh = [], [], []
    for j in range(tiles):
        a = ue[j] - u[j]
        b = at(V, j, 1) - v[j]
        shear = (at(U, j, 1) - u[j]) + (ve[j] - v[j])
        div = a + b
        ten = a - b
        q = div * div + 0.25 * (ten * ten + shear * shear) + 0.01
        s = at(S, j)
        t = s * lax.rsqrt(q)
        t4 = 0.25 * t
        g = t * div - s
        h = t4 * ten
        n1.append(KEEP * at(N1, j) + (g + h))
        n2.append(KEEP * at(N2, j) + (g - h))
        sh.append(KEEP * at(SH, j) + t4 * shear)
    for j in range(tiles):
        F[N1][j, pl.ds(r, n), :] = n1[j]
        F[N2][j, pl.ds(r, n), :] = n2[j]
        F[SH][j, pl.ds(r, n), :] = sh[j]
    n1w, shw = beside(n1, -1), beside(sh, -1)
    for j in range(tiles):
        fx = (n1[j] - n1w[j]) + (sh[j] - at(SH, j, -1))
        fy = (sh[j] - shw[j]) + (n2[j] - at(N2, j, -1))
        w = at(B, j)
        x = u[j] + 0.3 * v[j]
        y = v[j] - 0.3 * u[j]
        F[U][j, pl.ds(r, n), :] = (x + at(DE, j)) + w * (fx - x)
        F[V][j, pl.ds(r, n), :] = (y + at(DN, j)) + w * (fy - y)


def subcycles_inside(F):
    def one(_, carry):
        def rows(i, c):
            for t in range(4):
                subcycle_rows(F, pl.multiple_of(TOP + 64 * i + 16 * t, 8), 16)
            return c

        lax.fori_loop(0, ROWS // 64, rows, 0)
        return carry

    lax.fori_loop(0, SUBCYCLES, one, 0)


def subcycles_edges(T, G):
    def one(_, carry):
        subcycle_rows(T, 8, 32)
        for t in range(3):
            subcycle_rows(G, TOP - 8 + 48 * t, 48)
        return carry

    lax.fori_loop(0, SUBCYCLES, one, 0)


def merge_edges(F, T, G, fields):
    low = sublanes() < 4
    for f in fields:
        for j in range(4):
            first, last = pl.ds(TOP, 8), pl.ds(TOP + ROWS - 8, 8)
            F[f][j, first, :] = jnp.where(low, T[f][j, pl.ds(16, 8), :], F[f][j, first, :])
            F[f][j, last, :] = jnp.where(low, F[f][j, last, :], T[f][j, pl.ds(24, 8), :])
        n = 64
        for i in range(ROWS // n):
            at = pl.ds(TOP + i * n, n)
            lane = lanes(n)
            x = G[f][0, at, :]
            F[f][0, at, :] = jnp.where(lane < 4, x, F[f][0, at, :])
            F[f][3, at, :] = jnp.where(lane >= 124, pltpu.roll(x, 64, 1), F[f][3, at, :])


def placing(own, place):
    owner = jnp.concatenate(
        [jnp.broadcast_to(own[:, c : c + 1], (8, 128)) for c in range(32)], axis=0
    )
    hot = jnp.where(owner == lanes(256), 1.0, 0.0)
    row = lax.broadcasted_iota(jnp.int32, (256, 256), 0)
    col = lax.broadcasted_iota(jnp.int32, (256, 256), 1)
    before = (col % 8) * 32 + col // 8 < (row % 8) * 32 + row // 8
    before = jnp.where(before, 1.0, 0.0).astype(jnp.bfloat16)
    ranks = jnp.dot(before, hot.astype(jnp.bfloat16), preferred_element_type=jnp.float32)
    rank = jnp.sum(hot * ranks, axis=1, keepdims=True)
    slot = owner.astype(jnp.float32) * 16.0 + rank
    slot = jnp.concatenate([slot, slot], axis=1)
    chosen = jnp.where(slot == col.astype(jnp.float32), 1.0, 0.0)
    place[...] = chosen.T.astype(jnp.bfloat16)


def flatten_blocks(F, blocks):
    group = lanes() // 16
    odd = [(group // 2**t) % 2 == 1 for t in range(3)]
    for c in (U, V):
        for j in range(4):
            for h in range(2):
                x = [F[c][j, pl.ds(TOP + 8 * h + r, 8, stride=16), :] for r in range(8)]
                x = [pltpu.roll(y, 16 * r, 1) if r else y for r, y in enumerate(x)]
                for t in range(3):
                    x = [jnp.where(odd[t], x[(m + 2**t) % 8], x[m]) for m in range(8)]
                for b in range(8):
                    y = x[(8 - b) % 8]
                    y = pltpu.roll(y, 128 - 16 * b, 1) if b else y
                    blocks[pl.ds((8 * j + b) * 8, 8), pl.ds((2 * c + h) * 128, 128)] = y


def gather_blocks(place, blocks, send):
    p = place[...]
    for c in range(2):
        x = blocks[:, pl.ds(256 * c, 256)]
        out = None
        for _ in range(3):
            part = x.astype(jnp.bfloat16)
            term = jnp.dot(p, part, preferred_element_type=jnp.float32)
            out = term if out is None else out + term
            x = x - part.astype(jnp.float32)
        send[c] = out


def dynamics(
    vol_ref, area_ref, vel_ref, forc_ref, cur_ref, strs_ref, mask_ref, own_ref,
    stress_out, vel_out,
    held, mask, own,
    f0, f1, f2, f3, f4, f5, f6, f7, f8,
    t0, t1, t2, t3, t4, t5, t6, t7, t8,
    g0, g1, g2, g3, g4, g5, g6, g7, g8,
    W, WE, WW, send_n, send_s, recv_s, recv_n,
    place, blocks, send,
    in_sem, halo_send, halo_recv, out_sem,
):
    F = (f0, f1, f2, f3, f4, f5, f6, f7, f8)
    T = (t0, t1, t2, t3, t4, t5, t6, t7, t8)
    G = (g0, g1, g2, g3, g4, g5, g6, g7, g8)
    gx, gy = lax.axis_index("gx"), lax.axis_index("gy")
    n_gx, n_gy = lax.axis_size("gx"), lax.axis_size("gy")
    east, west = lax.rem(gx + 1, n_gx), lax.rem(gx + n_gx - 1, n_gx)
    north, south = lax.rem(gy + 1, n_gy), lax.rem(gy + n_gy - 1, n_gy)

    has_e, has_w, has_n, has_s = gx < n_gx - 1, gx > 0, gy < n_gy - 1, gy > 0

    every, inner, mid = pl.ds(0, ROWS), pl.ds(8, ROWS - 16), pl.ds(128, COLS - 256)
    parts = (
        (every, pl.ds(0, 128)),
        (every, pl.ds(COLS - 128, 128)),
        (pl.ds(0, 8), mid),
        (pl.ds(ROWS - 8, 8), mid),
        (inner, mid),
    )
    sources = (vol_ref, area_ref, vel_ref, forc_ref, cur_ref, strs_ref)

    def start_load(k):
        r, c = parts[k]
        start = 0
        for src in sources:
            dst = held.at[pl.ds(start, src.shape[0]), r, c]
            pltpu.make_async_copy(src.at[:, r, c], dst, in_sem.at[k]).start()
            start += src.shape[0]

    def wait_load(k):
        at = held.at[:, parts[k][0], parts[k][1]]
        pltpu.make_async_copy(at, at, in_sem.at[k]).wait()

    masks = [
        pltpu.make_async_copy(mask_ref.at[:, c], mask.at[:, c], in_sem.at[5 + k])
        for k, c in enumerate((parts[0][1], parts[1][1], mid))
    ]
    own_load = pltpu.make_async_copy(own_ref, own, in_sem.at[8])
    start_load(0)
    masks[0].start()
    start_load(1)
    masks[1].start()

    barrier = pltpu.get_barrier_semaphore()
    around = (
        (has_e, (east, gy)),
        (has_w, (west, gy)),
        (has_e & has_n, (east, north)),
        (has_e & has_s, (east, south)),
        (has_w & has_n, (west, north)),
        (has_w & has_s, (west, south)),
    )
    for there, device in around:

        @pl.when(there)
        def _(device=device):
            pl.semaphore_signal(barrier, inc=1, device_id=device, device_id_type=MESH)

    for k in range(1, 16):
        pl.semaphore_signal(
            barrier, inc=1, device_id=(gx, lax.rem(gy + k, n_gy)), device_id_type=MESH
        )
    one, zero = jnp.int32(1), jnp.int32(0)
    count = lambda there: jnp.where(there, one, zero)
    greeted = 15 + (count(has_e) + count(has_w)) * (1 + count(has_n) + count(has_s))

    start_load(2)
    start_load(3)
    masks[2].start()
    start_load(4)
    own_load.start()

    for buf, tiles, ends in ((F, 4, (8, 144)), (T, 4, (0, 40)), (G, 1, (0, 152))):
        for f in buf:
            for j in range(tiles):
                for r in ends:
                    f[j, pl.ds(r, 8), :] = jnp.zeros((8, 128), jnp.float32)
    above, below, same = pl.ds(TOP + ROWS, 8), pl.ds(TOP - 8, 8), pl.ds(TOP, ROWS)
    for there, buf in ((has_s, recv_s), (has_n, recv_n)):

        @pl.when(jnp.logical_not(there))
        def _(buf=buf):
            buf[...] = jnp.zeros(buf.shape, jnp.float32)

    for there, buf in ((has_e, WE), (has_w, WW)):
        for beside, at in ((has_n, above), (has_s, below), (there, same)):

            @pl.when(jnp.logical_not(there & beside))
            def _(buf=buf, at=at):
                buf[at, :] = jnp.zeros((at.size, 128), jnp.float32)

    first, last = W.at[pl.ds(0, 8), :], W.at[pl.ds(ROWS - 8, 8), :]
    halos = (
        (send_n, recv_s, (gx, north), has_n, has_s),
        (send_s, recv_n, (gx, south), has_s, has_n),
        (W, WW.at[same, :], (east, gy), has_e, has_w),
        (W, WE.at[same, :], (west, gy), has_w, has_e),
        (first, WW.at[above, :], (east, south), has_e & has_s, has_w & has_n),
        (first, WE.at[above, :], (west, south), has_w & has_s, has_e & has_n),
        (last, WW.at[below, :], (east, north), has_e & has_n, has_w & has_s),
        (last, WE.at[below, :], (west, north), has_w & has_n, has_e & has_s),
    )

    def halo(k):
        src, dst, device, _, _ = halos[k]
        return pltpu.make_async_remote_copy(
            src_ref=src,
            dst_ref=dst,
            send_sem=halo_send.at[k],
            recv_sem=halo_recv.at[k],
            device_id=device,
            device_id_type=MESH,
        )

    def start_halo(k):
        @pl.when(halos[k][3])
        def _():
            halo(k).start()

    wait_load(0)
    masks[0].wait()
    wait_load(1)
    masks[1].wait()
    prepare((held, mask), F, 0, 2, 64, 64, (0, 3))
    pack_lon(F, W)
    pl.semaphore_wait(barrier, greeted)
    for k in range(2, 8):
        start_halo(k)

    wait_load(2)
    wait_load(3)
    masks[2].wait()
    prepare((held, mask), F, 0, 2, ROWS - 8, 8, (1, 2))
    pack_lat(F, send_n, send_s)
    for k in (0, 1):
        start_halo(k)

    wait_load(4)
    prepare((held, mask), F, 8, 2, 56, 56, (1, 2))
    copy_edges(F, T, G)
    subcycles_inside(F)
    own_load.wait()
    placing(own, place)

    for k in range(8):

        @pl.when(halos[k][4])
        def _(k=k):
            halo(k).wait_recv()

    unpack_lat(T, G, recv_s, recv_n)
    unpack_lon(G, WE, WW)
    subcycles_edges(T, G)
    merge_edges(F, T, G, (U, V))
    flatten_blocks(F, blocks)
    gather_blocks(place, blocks, send)

    z, x = gy // 4, lax.rem(gy, 4)
    mine = pl.ds(pl.multiple_of(gy * 16, 16), 16)
    for dz, dx in PEERS:
        to = lax.rem(z + dz, 4) * 4 + lax.rem(x + dx, 4)
        copy = pltpu.make_async_remote_copy(
            src_ref=send.at[:, pl.ds(pl.multiple_of(to * 16, 16), 16), :],
            dst_ref=vel_out.at[:, mine, :],
            send_sem=out_sem.at[0],
            recv_sem=out_sem.at[1],
            device_id=(gx, to),
            device_id_type=MESH,
        )
        copy.start()
    local = pltpu.make_async_copy(send.at[:, mine, :], vel_out.at[:, mine, :], out_sem.at[2])
    local.start()

    merge_edges(F, T, G, (N1, N2, SH))

    def rows(i, carry):
        src = pl.ds(pl.multiple_of(i * 16 + TOP, 8), 16)
        dst = pl.ds(pl.multiple_of(i * 16, 8), 16)
        for j in range(4):
            col = pl.ds(j * 128, 128)
            stress_out[0, dst, col] = 0.5 * (F[N1][j, src, :] + F[N2][j, src, :])
            stress_out[1, dst, col] = 0.5 * (F[N1][j, src, :] - F[N2][j, src, :])
            stress_out[2, dst, col] = 0.5 * F[SH][j, src, :]
        return carry

    lax.fori_loop(0, ROWS // 16, rows, 0)

    for k in range(8):

        @pl.when(halos[k][3])
        def _(k=k):
            halo(k).wait_send()

    others = pl.ds(0, 240)
    for k in range(2):
        pltpu.make_async_copy(send.at[:, others, :], vel_out.at[:, others, :], out_sem.at[k]).wait()
    local.wait()


def write_out(stress, vel, stress_out, vel_out, sem):
    copies = [
        pltpu.make_async_copy(stress, stress_out, sem.at[0]),
        pltpu.make_async_copy(vel, vel_out, sem.at[1]),
    ]
    for copy in copies:
        copy.start()
    for copy in copies:
        copy.wait()


def per_device(ice_volume, ice_area, velocity, forcing, current, stress, ice_mask, block_owner):
    f32, dma, vmem = jnp.float32, pltpu.SemaphoreType.DMA, pltpu.VMEM
    args = (ice_volume, ice_area, velocity, forcing, current, stress, ice_mask, block_owner)
    args = [pltpu.with_memory_space_constraint(a, pltpu.HBM) for a in args]
    stress_shape, vel_shape = (3, ROWS, COLS), (2, 256, 256)
    scratch = [vmem((19, ROWS, COLS), f32)] + [vmem(a.shape, a.dtype) for a in args[6:]]
    scratch += [vmem((4, HIGH, 128), f32)] * 9 + [vmem((4, 48, 128), f32)] * 9
    scratch += [vmem((1, HIGH, 128), f32)] * 9
    scratch += [vmem((ROWS, 128), f32), vmem((HIGH, 128), f32), vmem((HIGH, 128), f32)]
    scratch += [vmem((5, 4, 8, 128), f32)] * 4
    scratch += [vmem((256, 256), jnp.bfloat16), vmem((256, 512), f32), vmem(vel_shape, f32)]
    scratch += [dma((9,)), dma((8,)), dma((8,)), dma((3,))]
    held_stress, held_vel = pl.pallas_call(
        dynamics,
        out_shape=(vmem(stress_shape, f32), vmem(vel_shape, f32)),
        in_specs=[pl.BlockSpec(memory_space=pltpu.HBM)] * 8,
        out_specs=(pl.BlockSpec(memory_space=vmem),) * 2,
        scratch_shapes=scratch,
        compiler_params=pltpu.CompilerParams(
            collective_id=0, has_side_effects=True, vmem_limit_bytes=48 * 2**20
        ),
    )(*args)
    held_stress = pltpu.with_memory_space_constraint(held_stress, vmem)
    held_vel = pltpu.with_memory_space_constraint(held_vel, vmem)
    stress_out, vel_out = pl.pallas_call(
        write_out,
        out_shape=(
            jax.ShapeDtypeStruct(stress_shape, f32),
            jax.ShapeDtypeStruct(vel_shape, f32),
        ),
        in_specs=[pl.BlockSpec(memory_space=vmem)] * 2,
        out_specs=(pl.BlockSpec(memory_space=pl.ANY),) * 2,
        scratch_shapes=[dma((2,))],
    )(held_stress, held_vel)
    return (stress_out, vel_out[:, None])


def solution(mesh):
    tile = P(None, "gy", "gx")
    in_specs = (tile,) * 6 + (P("gy", "gx"),) * 2
    out_specs = (tile, P(None, "gx", "gy", None))
    return jax.shard_map(
        per_device, mesh=mesh, in_specs=in_specs, out_specs=out_specs, check_vma=False
    )
```

```python
import functools

import jax
import jax.numpy as jnp
from jax import lax
from jax.experimental import pallas as pl
from jax.experimental.pallas import tpu as pltpu
from jax.sharding import PartitionSpec as P

MESH = pl.DeviceIdType.MESH
BLOCK = 16
SUBCYCLES = 4
ROWS, COLS = 128, 512
TOP = 16
HIGH = ROWS + 32
KEEP = 2.0 / 3.0
OWNERS = (0, 1, 4, 3, 2, 5, 8, 7, 6, 9, 12, 11, 10, 13, 15, 14)
U, V, N1, N2, SH, S, B, DE, DN = range(9)


def lanes(n=8):
    return lax.broadcasted_iota(jnp.int32, (n, 128), 1)


def sublanes():
    return lax.broadcasted_iota(jnp.int32, (8, 128), 0)


def prepare(raw, F, first, count, step, n, tiles):
    held, mask = raw
    vol, area, vel = held.at[0:5], held.at[5:10], held.at[10:12]
    forc, cur, strs = held.at[12:14], held.at[14:16], held.at[16:19]

    def rows(i, carry):
        row = first + step * i
        src = pl.ds(pl.multiple_of(row, 8), n)
        dst = pl.ds(pl.multiple_of(row + TOP, 8), n)
        for j in tiles:
            col = pl.ds(j * 128, 128)
            m = mask[src, col].astype(jnp.float32)
            v = [vol[c, src, col] for c in range(5)]
            a = [area[c, src, col] for c in range(5)]
            total = ((v[0] + v[1]) + (v[2] + v[3])) + v[4]
            conc = ((a[0] + a[1]) + (a[2] + a[3])) + a[4]
            strength = 2.0 * total * jnp.exp(-20.0 * (1.0 - conc))
            weight = m / (total + 1.0)
            F[S][j, dst, :] = strength * m * (1.0 / 3.0)
            F[B][j, dst, :] = 0.5 * weight
            F[DE][j, dst, :] = weight * (forc[0, src, col] + 0.5 * cur[0, src, col])
            F[DN][j, dst, :] = weight * (forc[1, src, col] + 0.5 * cur[1, src, col])
            F[U][j, dst, :] = vel[0, src, col] * m
            F[V][j, dst, :] = vel[1, src, col] * m
            F[N1][j, dst, :] = m * (strs[0, src, col] + strs[1, src, col])
            F[N2][j, dst, :] = m * (strs[0, src, col] - strs[1, src, col])
            F[SH][j, dst, :] = (m + m) * strs[2, src, col]
        return carry

    lax.fori_loop(0, count, rows, 0, unroll=count == 2 and n == 8)


def pack_lon(F, W, start, n):
    lane = lanes(n)
    src = pl.ds(start + TOP, n)
    out = jnp.zeros((n, 128), jnp.float32)
    for f in range(9):
        x = jnp.where(lane < 64, F[f][0, src, :], F[f][3, src, :])
        x = pltpu.roll(x, 8 * f, 1) if f else x
        here = (lane < 8 * f + 4) & (lane >= 8 * f - 4) if f else (lane < 4) | (lane >= 124)
        out = jnp.where(here, x, out)
    W[pl.ds(start, n), :] = out


def pack_lat(F, send_n, send_s):
    low = sublanes() < 4
    for p in range(5):
        f, g = 2 * p, min(2 * p + 1, 8)
        for j in range(4):
            last = pl.ds(TOP + ROWS - 8, 8)
            first = pl.ds(TOP, 8)
            send_n[p, j] = jnp.where(low, pltpu.roll(F[f][j, last, :], 4, 0), F[g][j, last, :])
            send_s[p, j] = jnp.where(low, F[f][j, first, :], pltpu.roll(F[g][j, first, :], 4, 0))


def turn(x, by):
    return pltpu.roll(x, by % 128, 1) if by % 128 else x


def edge_columns(first, last, q):
    lane = lanes(first.shape[0])
    in_east = (lane >= 32 * q) & (lane < 32 * q + 8)
    in_west = (lane >= 32 * q + 24) & (lane < 32 * q + 32)
    return in_east, turn(last, 32 * q + 8), in_west, turn(first, 32 * q + 24)


def copy_edges(F, T, G):
    for f in range(9):
        for j in range(4):
            T[f][j, pl.ds(12, 8), :] = F[f][j, pl.ds(TOP, 8), :]
            T[f][j, pl.ds(20, 8), :] = F[f][j, pl.ds(TOP + ROWS - 8, 8), :]
        out = jnp.zeros((40, 128), jnp.float32)
        for q in range(4):
            at = pl.ds(TOP - 4 + 32 * q, 40)
            in_east, east, in_west, west = edge_columns(F[f][0, at, :], F[f][3, at, :], q)
            out = jnp.where(in_east, east, jnp.where(in_west, west, out))
        G[f][0, pl.ds(8, 40), :] = out


def unpack_lat(T, G, recv_s, recv_n):
    for f in range(9):
        half = pl.ds(4 * (f % 2), 4)
        for j in range(4):
            T[f][j, pl.ds(8, 4), :] = recv_s[f // 2, j, half, :]
            T[f][j, pl.ds(28, 4), :] = recv_n[f // 2, j, half, :]
        for q, src, dst in ((0, pl.ds(8, 4), pl.ds(8, 4)), (3, pl.ds(28, 4), pl.ds(44, 4))):
            in_east, east, in_west, west = edge_columns(T[f][0, src, :], T[f][3, src, :], q)
            own = jnp.where(in_west, west, G[f][0, dst, :])
            G[f][0, dst, :] = jnp.where(in_east, east, own)


def unpack_lon(G, WE, WW):
    n = 40
    lane = lanes(n)
    ahead = lane % 8 < 4
    x = []
    for q in range(4):
        at = pl.ds(TOP - 4 + 32 * q, n)
        x.append(jnp.where(ahead, pltpu.roll(WE[at, :], 112, 1), WW[at, :]))
    for f in range(9):
        out = G[f][0, pl.ds(8, n), :]
        for q in range(4):
            in_east = (lane >= 32 * q + 8) & (lane < 32 * q + 12)
            in_west = (lane >= 32 * q + 20) & (lane < 32 * q + 24)
            out = jnp.where(in_east | in_west, turn(x[q], 32 * q + 24 - 8 * f), out)
        G[f][0, pl.ds(8, n), :] = out


def subcycle_rows(F, r, n):
    tiles = F[0].shape[0]
    lane = lanes(n)
    not_last, not_first = lane < 127, lane > 0
    at = lambda f, j, off=0: F[f][j, pl.ds(r + off, n), :]

    def beside(x, step):
        turned = [pltpu.roll(y, 127 if step > 0 else 1, 1) for y in x]
        if tiles == 1:
            return turned
        inside = not_last if step > 0 else not_first
        return [jnp.where(inside, turned[j], turned[(j + step) % tiles]) for j in range(tiles)]

    u = [at(U, j) for j in range(tiles)]
    v = [at(V, j) for j in range(tiles)]
    ue, ve = beside(u, 1), beside(v, 1)
    n1, n2, sh = [], [], []
    for j in range(tiles):
        a = ue[j] - u[j]
        b = at(V, j, 1) - v[j]
        shear = (at(U, j, 1) - u[j]) + (ve[j] - v[j])
        div = a + b
        ten = a - b
        q = div * div + 0.25 * (ten * ten + shear * shear) + 0.01
        s = at(S, j)
        t = s * lax.rsqrt(q)
        t4 = 0.25 * t
        g = t * div - s
        h = t4 * ten
        n1.append(KEEP * at(N1, j) + (g + h))
        n2.append(KEEP * at(N2, j) + (g - h))
        sh.append(KEEP * at(SH, j) + t4 * shear)
    for j in range(tiles):
        F[N1][j, pl.ds(r, n), :] = n1[j]
        F[N2][j, pl.ds(r, n), :] = n2[j]
        F[SH][j, pl.ds(r, n), :] = sh[j]
    n1w, shw = beside(n1, -1), beside(sh, -1)
    for j in range(tiles):
        fx = (n1[j] - n1w[j]) + (sh[j] - at(SH, j, -1))
        fy = (sh[j] - shw[j]) + (n2[j] - at(N2, j, -1))
        w = at(B, j)
        x = u[j] + 0.3 * v[j]
        y = v[j] - 0.3 * u[j]
        F[U][j, pl.ds(r, n), :] = (x + at(DE, j)) + w * (fx - x)
        F[V][j, pl.ds(r, n), :] = (y + at(DN, j)) + w * (fy - y)


def subcycles_inside(F):
    def one(_, carry):
        def rows(i, c):
            for t in range(4):
                subcycle_rows(F, pl.multiple_of(TOP + 64 * i + 16 * t, 8), 16)
            return c

        lax.fori_loop(0, ROWS // 64, rows, 0)
        return carry

    lax.fori_loop(0, SUBCYCLES, one, 0)


def subcycles_edges(T, G):
    def one(_, carry):
        subcycle_rows(T, 8, 24)
        subcycle_rows(G, 8, 40)
        return carry

    lax.fori_loop(0, SUBCYCLES, one, 0)


def merge_edges(F, T, G, fields):
    n = 32
    lane = lanes(n)
    for f in fields:
        for j in range(4):
            F[f][j, pl.ds(TOP, 4), :] = T[f][j, pl.ds(12, 4), :]
            F[f][j, pl.ds(TOP + ROWS - 4, 4), :] = T[f][j, pl.ds(24, 4), :]
        x = G[f][0, pl.ds(12, n), :]
        for q in range(4):
            at = pl.ds(TOP + n * q, n)
            F[f][0, at, :] = jnp.where(lane < 4, turn(x, -32 * q - 24), F[f][0, at, :])
            F[f][3, at, :] = jnp.where(lane >= 124, turn(x, 120 - 32 * q), F[f][3, at, :])


def placing(own, place):
    owner = jnp.concatenate(
        [jnp.broadcast_to(own[:, c : c + 1], (8, 128)) for c in range(32)], axis=0
    )
    hot = jnp.where(owner == lanes(256), 1.0, 0.0)
    row = lax.broadcasted_iota(jnp.int32, (256, 256), 0)
    col = lax.broadcasted_iota(jnp.int32, (256, 256), 1)
    before = (col % 8) * 32 + col // 8 < (row % 8) * 32 + row // 8
    before = jnp.where(before, 1.0, 0.0).astype(jnp.bfloat16)
    ranks = jnp.dot(before, hot.astype(jnp.bfloat16), preferred_element_type=jnp.float32)
    rank = jnp.sum(hot * ranks, axis=1, keepdims=True)
    slot = owner.astype(jnp.float32) * 16.0 + rank
    slot = jnp.concatenate([slot, slot], axis=1)
    chosen = jnp.where(slot == col.astype(jnp.float32), 1.0, 0.0)
    place[...] = chosen.T.astype(jnp.bfloat16)


def flatten_blocks(F, blocks):
    group = lanes() // 16
    odd = [(group // 2**t) % 2 == 1 for t in range(3)]
    for c in (U, V):
        for j in range(4):
            for h in range(2):
                x = [F[c][j, pl.ds(TOP + 8 * h + r, 8, stride=16), :] for r in range(8)]
                x = [pltpu.roll(y, 16 * r, 1) if r else y for r, y in enumerate(x)]
                for t in range(3):
                    x = [jnp.where(odd[t], x[(m + 2**t) % 8], x[m]) for m in range(8)]
                for b in range(8):
                    y = x[(8 - b) % 8]
                    y = pltpu.roll(y, 128 - 16 * b, 1) if b else y
                    blocks[pl.ds((8 * j + b) * 8, 8), pl.ds((2 * c + h) * 128, 128)] = y


def gather_blocks(place, blocks, send):
    p = place[...]
    for c in range(2):
        x = blocks[:, pl.ds(256 * c, 256)]
        out = None
        for _ in range(3):
            part = x.astype(jnp.bfloat16)
            term = jnp.dot(p, part, preferred_element_type=jnp.float32)
            out = term if out is None else out + term
            x = x - part.astype(jnp.float32)
        send[c] = out


def dynamics(
    vol_ref, area_ref, vel_ref, forc_ref, cur_ref, strs_ref, mask_ref, own_ref,
    stress_out, vel_out,
    held, mask, own,
    f0, f1, f2, f3, f4, f5, f6, f7, f8,
    t0, t1, t2, t3, t4, t5, t6, t7, t8,
    g0, g1, g2, g3, g4, g5, g6, g7, g8,
    W, WE, WW, send_n, send_s, recv_s, recv_n,
    place, blocks, send,
    in_sem, halo_send, halo_recv, out_sem,
):
    F = (f0, f1, f2, f3, f4, f5, f6, f7, f8)
    T = (t0, t1, t2, t3, t4, t5, t6, t7, t8)
    G = (g0, g1, g2, g3, g4, g5, g6, g7, g8)
    gx, gy = lax.axis_index("gx"), lax.axis_index("gy")
    n_gx, n_gy = lax.axis_size("gx"), lax.axis_size("gy")
    east, west = lax.rem(gx + 1, n_gx), lax.rem(gx + n_gx - 1, n_gx)
    north, south = lax.rem(gy + 1, n_gy), lax.rem(gy + n_gy - 1, n_gy)

    has_e, has_w, has_n, has_s = gx < n_gx - 1, gx > 0, gy < n_gy - 1, gy > 0

    upper, lower = pl.ds(0, 64), pl.ds(64, 64)
    inner, mid = pl.ds(8, ROWS - 16), pl.ds(128, COLS - 256)
    left, right = pl.ds(0, 128), pl.ds(COLS - 128, 128)
    parts = (
        (upper, left),
        (upper, right),
        (lower, left),
        (lower, right),
        (pl.ds(0, 8), mid),
        (pl.ds(ROWS - 8, 8), mid),
        (inner, mid),
    )
    sources = (vol_ref, area_ref, vel_ref, forc_ref, cur_ref, strs_ref)

    def start_load(k):
        r, c = parts[k]
        start = 0
        for src in sources:
            dst = held.at[pl.ds(start, src.shape[0]), r, c]
            pltpu.make_async_copy(src.at[:, r, c], dst, in_sem.at[k]).start()
            start += src.shape[0]

    def wait_load(k):
        at = held.at[:, parts[k][0], parts[k][1]]
        pltpu.make_async_copy(at, at, in_sem.at[k]).wait()

    masks = [
        pltpu.make_async_copy(mask_ref.at[:, c], mask.at[:, c], in_sem.at[7 + k])
        for k, c in enumerate((left, right, mid))
    ]
    own_load = pltpu.make_async_copy(own_ref, own, in_sem.at[10])
    own_load.start()
    masks[0].start()
    masks[1].start()
    start_load(0)
    start_load(1)

    barrier = pltpu.get_barrier_semaphore()
    around = (
        (has_e, (east, gy)),
        (has_w, (west, gy)),
        (has_e & has_n, (east, north)),
        (has_e & has_s, (east, south)),
        (has_w & has_n, (west, north)),
        (has_w & has_s, (west, south)),
    )
    for there, device in around:

        @pl.when(there)
        def _(device=device):
            pl.semaphore_signal(barrier, inc=1, device_id=device, device_id_type=MESH)

    for k in range(1, 16):
        pl.semaphore_signal(
            barrier, inc=1, device_id=(gx, lax.rem(gy + k, n_gy)), device_id_type=MESH
        )
    one, zero = jnp.int32(1), jnp.int32(0)
    count = lambda there: jnp.where(there, one, zero)
    greeted = 15 + (count(has_e) + count(has_w)) * (1 + count(has_n) + count(has_s))

    start_load(2)
    start_load(3)
    start_load(4)
    start_load(5)
    masks[2].start()
    start_load(6)

    for buf, tiles, ends in ((F, 4, (8, 144)), (T, 4, (0, 32)), (G, 1, (0, 48))):
        for f in buf:
            for j in range(tiles):
                for r in ends:
                    f[j, pl.ds(r, 8), :] = jnp.zeros((8, 128), jnp.float32)
    above, below, same = pl.ds(TOP + ROWS, 8), pl.ds(TOP - 8, 8), pl.ds(TOP, ROWS)
    for there, buf in ((has_s, recv_s), (has_n, recv_n)):

        @pl.when(jnp.logical_not(there))
        def _(buf=buf):
            buf[...] = jnp.zeros(buf.shape, jnp.float32)

    for there, buf in ((has_e, WE), (has_w, WW)):
        for beside, at in ((has_n, above), (has_s, below), (there, same)):

            @pl.when(jnp.logical_not(there & beside))
            def _(buf=buf, at=at):
                buf[at, :] = jnp.zeros((at.size, 128), jnp.float32)

    first, last = W.at[pl.ds(0, 8), :], W.at[pl.ds(ROWS - 8, 8), :]
    halos = (
        (send_n, recv_s, (gx, north), has_n, has_s),
        (send_s, recv_n, (gx, south), has_s, has_n),
        (W, WW.at[same, :], (east, gy), has_e, has_w),
        (W, WE.at[same, :], (west, gy), has_w, has_e),
        (first, WW.at[above, :], (east, south), has_e & has_s, has_w & has_n),
        (first, WE.at[above, :], (west, south), has_w & has_s, has_e & has_n),
        (last, WW.at[below, :], (east, north), has_e & has_n, has_w & has_s),
        (last, WE.at[below, :], (west, north), has_w & has_n, has_e & has_s),
    )

    def halo(k):
        src, dst, device, _, _ = halos[k]
        return pltpu.make_async_remote_copy(
            src_ref=src,
            dst_ref=dst,
            send_sem=halo_send.at[k],
            recv_sem=halo_recv.at[k],
            device_id=device,
            device_id_type=MESH,
        )

    def start_halo(k):
        @pl.when(halos[k][3])
        def _():
            halo(k).start()

    own_load.wait()
    placing(own, place)

    masks[0].wait()
    masks[1].wait()
    for half in range(2):
        wait_load(2 * half)
        wait_load(2 * half + 1)
        prepare((held, mask), F, 64 * half, 1, 0, 64, (0, 3))
        pack_lon(F, W, 64 * half, 64)
    pl.semaphore_wait(barrier, greeted)
    for k in range(2, 8):
        start_halo(k)

    wait_load(4)
    wait_load(5)
    masks[2].wait()
    prepare((held, mask), F, 0, 2, ROWS - 8, 8, (1, 2))
    pack_lat(F, send_n, send_s)
    for k in (0, 1):
        start_halo(k)

    wait_load(6)
    prepare((held, mask), F, 8, 2, 56, 56, (1, 2))
    copy_edges(F, T, G)
    subcycles_inside(F)

    for k in range(8):

        @pl.when(halos[k][4])
        def _(k=k):
            halo(k).wait_recv()

    unpack_lat(T, G, recv_s, recv_n)
    unpack_lon(G, WE, WW)
    subcycles_edges(T, G)
    merge_edges(F, T, G, (U, V))
    flatten_blocks(F, blocks)
    gather_blocks(place, blocks, send)

    mine = pl.ds(pl.multiple_of(gy * 16, 16), 16)
    for to in OWNERS:

        @pl.when(gy != to)
        def _(to=to):
            pltpu.make_async_remote_copy(
                src_ref=send.at[:, pl.ds(pl.multiple_of(to * 16, 16), 16), :],
                dst_ref=vel_out.at[:, mine, :],
                send_sem=out_sem.at[0],
                recv_sem=out_sem.at[1],
                device_id=(gx, to),
                device_id_type=MESH,
            ).start()

    local = pltpu.make_async_copy(send.at[:, mine, :], vel_out.at[:, mine, :], out_sem.at[2])
    local.start()

    merge_edges(F, T, G, (N1, N2, SH))

    def rows(i, carry):
        src = pl.ds(pl.multiple_of(i * 16 + TOP, 8), 16)
        dst = pl.ds(pl.multiple_of(i * 16, 8), 16)
        for j in range(4):
            col = pl.ds(j * 128, 128)
            stress_out[0, dst, col] = 0.5 * (F[N1][j, src, :] + F[N2][j, src, :])
            stress_out[1, dst, col] = 0.5 * (F[N1][j, src, :] - F[N2][j, src, :])
            stress_out[2, dst, col] = 0.5 * F[SH][j, src, :]
        return carry

    lax.fori_loop(0, ROWS // 16, rows, 0)

    for k in range(8):

        @pl.when(halos[k][3])
        def _(k=k):
            halo(k).wait_send()

    others = pl.ds(0, 240)
    for k in range(2):
        pltpu.make_async_copy(send.at[:, others, :], vel_out.at[:, others, :], out_sem.at[k]).wait()
    local.wait()


def write_out(stress, vel, stress_out, vel_out, sem):
    copies = [
        pltpu.make_async_copy(stress, stress_out, sem.at[0]),
        pltpu.make_async_copy(vel, vel_out, sem.at[1]),
    ]
    for copy in copies:
        copy.start()
    for copy in copies:
        copy.wait()


def per_device(ice_volume, ice_area, velocity, forcing, current, stress, ice_mask, block_owner):
    f32, dma, vmem = jnp.float32, pltpu.SemaphoreType.DMA, pltpu.VMEM
    args = (ice_volume, ice_area, velocity, forcing, current, stress, ice_mask, block_owner)
    args = [pltpu.with_memory_space_constraint(a, pltpu.HBM) for a in args]
    stress_shape, vel_shape = (3, ROWS, COLS), (2, 256, 256)
    scratch = [vmem((19, ROWS, COLS), f32)] + [vmem(a.shape, a.dtype) for a in args[6:]]
    scratch += [vmem((4, HIGH, 128), f32)] * 9 + [vmem((4, 40, 128), f32)] * 9
    scratch += [vmem((1, 56, 128), f32)] * 9
    scratch += [vmem((ROWS, 128), f32), vmem((HIGH, 128), f32), vmem((HIGH, 128), f32)]
    scratch += [vmem((5, 4, 8, 128), f32)] * 4
    scratch += [vmem((256, 256), jnp.bfloat16), vmem((256, 512), f32), vmem(vel_shape, f32)]
    scratch += [dma((11,)), dma((8,)), dma((8,)), dma((3,))]
    held_stress, held_vel = pl.pallas_call(
        dynamics,
        out_shape=(vmem(stress_shape, f32), vmem(vel_shape, f32)),
        in_specs=[pl.BlockSpec(memory_space=pltpu.HBM)] * 8,
        out_specs=(pl.BlockSpec(memory_space=vmem),) * 2,
        scratch_shapes=scratch,
        compiler_params=pltpu.CompilerParams(
            collective_id=0, has_side_effects=True, vmem_limit_bytes=48 * 2**20
        ),
    )(*args)
    held_stress = pltpu.with_memory_space_constraint(held_stress, vmem)
    held_vel = pltpu.with_memory_space_constraint(held_vel, vmem)
    stress_out, vel_out = pl.pallas_call(
        write_out,
        out_shape=(
            jax.ShapeDtypeStruct(stress_shape, f32),
            jax.ShapeDtypeStruct(vel_shape, f32),
        ),
        in_specs=[pl.BlockSpec(memory_space=vmem)] * 2,
        out_specs=(pl.BlockSpec(memory_space=pl.ANY),) * 2,
        scratch_shapes=[dma((2,))],
    )(held_stress, held_vel)
    return (stress_out, vel_out[:, None])


def solution(mesh):
    tile = P(None, "gy", "gx")
    in_specs = (tile,) * 6 + (P("gy", "gx"),) * 2
    out_specs = (tile, P(None, "gx", "gy", None))
    return jax.shard_map(
        per_device, mesh=mesh, in_specs=in_specs, out_specs=out_specs, check_vma=False
    )
```

```python
import functools

import jax
import jax.numpy as jnp
from jax import lax
from jax.experimental import pallas as pl
from jax.experimental.pallas import tpu as pltpu
from jax.sharding import PartitionSpec as P

MESH = pl.DeviceIdType.MESH
BLOCK = 16
SUBCYCLES = 4
ROWS, COLS = 128, 512
TOP = 16
HIGH = ROWS + 32
KEEP = 2.0 / 3.0
OWNERS = (0, 1, 4, 3, 2, 5, 8, 7, 6, 9, 12, 11, 10, 13, 15, 14)
U, V, N1, N2, SH, S, B, DE, DN = range(9)


def lanes(n=8):
    return lax.broadcasted_iota(jnp.int32, (n, 128), 1)


def sublanes():
    return lax.broadcasted_iota(jnp.int32, (8, 128), 0)


def prepare(raw, F, first, count, step, n, tiles):
    held, mask = raw
    vol, area, vel = held.at[0:5], held.at[5:10], held.at[10:12]
    forc, cur, strs = held.at[12:14], held.at[14:16], held.at[16:19]

    def rows(i, carry):
        row = first + step * i
        src = pl.ds(pl.multiple_of(row, 8), n)
        dst = pl.ds(pl.multiple_of(row + TOP, 8), n)
        for j in tiles:
            col = pl.ds(j * 128, 128)
            m = mask[src, col].astype(jnp.float32)
            v = [vol[c, src, col] for c in range(5)]
            a = [area[c, src, col] for c in range(5)]
            total = ((v[0] + v[1]) + (v[2] + v[3])) + v[4]
            conc = ((a[0] + a[1]) + (a[2] + a[3])) + a[4]
            strength = 2.0 * total * jnp.exp(-20.0 * (1.0 - conc))
            weight = m / (total + 1.0)
            F[S][j, dst, :] = strength * m * (1.0 / 3.0)
            F[B][j, dst, :] = 0.5 * weight
            F[DE][j, dst, :] = weight * (forc[0, src, col] + 0.5 * cur[0, src, col])
            F[DN][j, dst, :] = weight * (forc[1, src, col] + 0.5 * cur[1, src, col])
            F[U][j, dst, :] = vel[0, src, col] * m
            F[V][j, dst, :] = vel[1, src, col] * m
            F[N1][j, dst, :] = m * (strs[0, src, col] + strs[1, src, col])
            F[N2][j, dst, :] = m * (strs[0, src, col] - strs[1, src, col])
            F[SH][j, dst, :] = (m + m) * strs[2, src, col]
        return carry

    lax.fori_loop(0, count, rows, 0, unroll=count == 2 and n == 8)


def pack_lon(F, W, start, n):
    lane = lanes(n)
    src = pl.ds(start + TOP, n)
    out = jnp.zeros((n, 128), jnp.float32)
    for f in range(9):
        x = jnp.where(lane < 64, F[f][0, src, :], F[f][3, src, :])
        x = pltpu.roll(x, 8 * f, 1) if f else x
        here = (lane < 8 * f + 4) & (lane >= 8 * f - 4) if f else (lane < 4) | (lane >= 124)
        out = jnp.where(here, x, out)
    W[pl.ds(start, n), :] = out


def pack_lat(F, send_n, send_s):
    low = sublanes() < 4
    for p in range(5):
        f, g = 2 * p, min(2 * p + 1, 8)
        for j in range(4):
            last = pl.ds(TOP + ROWS - 8, 8)
            first = pl.ds(TOP, 8)
            send_n[p, j] = jnp.where(low, pltpu.roll(F[f][j, last, :], 4, 0), F[g][j, last, :])
            send_s[p, j] = jnp.where(low, F[f][j, first, :], pltpu.roll(F[g][j, first, :], 4, 0))


def turn(x, by):
    return pltpu.roll(x, by % 128, 1) if by % 128 else x


def edge_columns(first, last, q):
    lane = lanes(first.shape[0])
    in_east = (lane >= 32 * q) & (lane < 32 * q + 8)
    in_west = (lane >= 32 * q + 24) & (lane < 32 * q + 32)
    return in_east, turn(last, 32 * q + 8), in_west, turn(first, 32 * q + 24)


def copy_edges(F, T, G):
    for f in range(9):
        for j in range(4):
            T[f][j, pl.ds(12, 8), :] = F[f][j, pl.ds(TOP, 8), :]
            T[f][j, pl.ds(20, 8), :] = F[f][j, pl.ds(TOP + ROWS - 8, 8), :]
        out = jnp.zeros((40, 128), jnp.float32)
        for q in range(4):
            at = pl.ds(TOP - 4 + 32 * q, 40)
            in_east, east, in_west, west = edge_columns(F[f][0, at, :], F[f][3, at, :], q)
            out = jnp.where(in_east, east, jnp.where(in_west, west, out))
        G[f][0, pl.ds(8, 40), :] = out


def unpack_lat(T, G, recv_s, recv_n):
    for f in range(9):
        half = pl.ds(4 * (f % 2), 4)
        for j in range(4):
            T[f][j, pl.ds(8, 4), :] = recv_s[f // 2, j, half, :]
            T[f][j, pl.ds(28, 4), :] = recv_n[f // 2, j, half, :]
        for q, src, dst in ((0, pl.ds(8, 4), pl.ds(8, 4)), (3, pl.ds(28, 4), pl.ds(44, 4))):
            in_east, east, in_west, west = edge_columns(T[f][0, src, :], T[f][3, src, :], q)
            own = jnp.where(in_west, west, G[f][0, dst, :])
            G[f][0, dst, :] = jnp.where(in_east, east, own)


def unpack_lon(G, WE, WW):
    n = 40
    lane = lanes(n)
    ahead = lane % 8 < 4
    x = []
    for q in range(4):
        at = pl.ds(TOP - 4 + 32 * q, n)
        x.append(jnp.where(ahead, pltpu.roll(WE[at, :], 112, 1), WW[at, :]))
    for f in range(9):
        out = G[f][0, pl.ds(8, n), :]
        for q in range(4):
            in_east = (lane >= 32 * q + 8) & (lane < 32 * q + 12)
            in_west = (lane >= 32 * q + 20) & (lane < 32 * q + 24)
            out = jnp.where(in_east | in_west, turn(x[q], 32 * q + 24 - 8 * f), out)
        G[f][0, pl.ds(8, n), :] = out


def subcycle_rows(F, r, n):
    tiles = F[0].shape[0]
    lane = lanes(n)
    not_last, not_first = lane < 127, lane > 0
    at = lambda f, j, off=0: F[f][j, pl.ds(r + off, n), :]

    def beside(x, step):
        turned = [pltpu.roll(y, 127 if step > 0 else 1, 1) for y in x]
        if tiles == 1:
            return turned
        inside = not_last if step > 0 else not_first
        return [jnp.where(inside, turned[j], turned[(j + step) % tiles]) for j in range(tiles)]

    u = [at(U, j) for j in range(tiles)]
    v = [at(V, j) for j in range(tiles)]
    ue, ve = beside(u, 1), beside(v, 1)
    n1, n2, sh = [], [], []
    for j in range(tiles):
        a = ue[j] - u[j]
        b = at(V, j, 1) - v[j]
        shear = (at(U, j, 1) - u[j]) + (ve[j] - v[j])
        div = a + b
        ten = a - b
        q = div * div + 0.25 * (ten * ten + shear * shear) + 0.01
        s = at(S, j)
        t = s * lax.rsqrt(q)
        t4 = 0.25 * t
        g = t * div - s
        h = t4 * ten
        n1.append(KEEP * at(N1, j) + (g + h))
        n2.append(KEEP * at(N2, j) + (g - h))
        sh.append(KEEP * at(SH, j) + t4 * shear)
    for j in range(tiles):
        F[N1][j, pl.ds(r, n), :] = n1[j]
        F[N2][j, pl.ds(r, n), :] = n2[j]
        F[SH][j, pl.ds(r, n), :] = sh[j]
    n1w, shw = beside(n1, -1), beside(sh, -1)
    for j in range(tiles):
        fx = (n1[j] - n1w[j]) + (sh[j] - at(SH, j, -1))
        fy = (sh[j] - shw[j]) + (n2[j] - at(N2, j, -1))
        w = at(B, j)
        x = u[j] + 0.3 * v[j]
        y = v[j] - 0.3 * u[j]
        F[U][j, pl.ds(r, n), :] = (x + at(DE, j)) + w * (fx - x)
        F[V][j, pl.ds(r, n), :] = (y + at(DN, j)) + w * (fy - y)


def subcycles_inside(F):
    def one(_, carry):
        def rows(i, c):
            for t in range(4):
                subcycle_rows(F, pl.multiple_of(TOP + 64 * i + 16 * t, 8), 16)
            return c

        lax.fori_loop(0, ROWS // 64, rows, 0)
        return carry

    lax.fori_loop(0, SUBCYCLES, one, 0)


def subcycles_edges(T, G):
    def one(_, carry):
        subcycle_rows(T, 8, 24)
        subcycle_rows(G, 8, 40)
        return carry

    lax.fori_loop(0, SUBCYCLES, one, 0, unroll=True)


def merge_edges(F, T, G, fields):
    n = 32
    lane = lanes(n)
    for f in fields:
        for j in range(4):
            F[f][j, pl.ds(TOP, 4), :] = T[f][j, pl.ds(12, 4), :]
            F[f][j, pl.ds(TOP + ROWS - 4, 4), :] = T[f][j, pl.ds(24, 4), :]
        x = G[f][0, pl.ds(12, n), :]
        for q in range(4):
            at = pl.ds(TOP + n * q, n)
            F[f][0, at, :] = jnp.where(lane < 4, turn(x, -32 * q - 24), F[f][0, at, :])
            F[f][3, at, :] = jnp.where(lane >= 124, turn(x, 120 - 32 * q), F[f][3, at, :])


def placing(own, place):
    owner = jnp.concatenate(
        [jnp.broadcast_to(own[:, c : c + 1], (8, 128)) for c in range(32)], axis=0
    )
    hot = jnp.where(owner == lanes(256), 1.0, 0.0)
    row = lax.broadcasted_iota(jnp.int32, (256, 256), 0)
    col = lax.broadcasted_iota(jnp.int32, (256, 256), 1)
    before = (col % 8) * 32 + col // 8 < (row % 8) * 32 + row // 8
    before = jnp.where(before, 1.0, 0.0).astype(jnp.bfloat16)
    ranks = jnp.dot(before, hot.astype(jnp.bfloat16), preferred_element_type=jnp.float32)
    rank = jnp.sum(hot * ranks, axis=1, keepdims=True)
    slot = owner.astype(jnp.float32) * 16.0 + rank
    slot = jnp.concatenate([slot, slot], axis=1)
    chosen = jnp.where(slot == col.astype(jnp.float32), 1.0, 0.0)
    place[...] = chosen.T.astype(jnp.bfloat16)


def flatten_blocks(F, blocks):
    group = lanes() // 16
    odd = [(group // 2**t) % 2 == 1 for t in range(3)]
    for c in (U, V):
        for j in range(4):
            for h in range(2):
                x = [F[c][j, pl.ds(TOP + 8 * h + r, 8, stride=16), :] for r in range(8)]
                x = [pltpu.roll(y, 16 * r, 1) if r else y for r, y in enumerate(x)]
                for t in range(3):
                    x = [jnp.where(odd[t], x[(m + 2**t) % 8], x[m]) for m in range(8)]
                for b in range(8):
                    y = x[(8 - b) % 8]
                    y = pltpu.roll(y, 128 - 16 * b, 1) if b else y
                    blocks[pl.ds((8 * j + b) * 8, 8), pl.ds((2 * c + h) * 128, 128)] = y


def gather_blocks(place, blocks, send):
    p = place[...]
    for c in range(2):
        x = blocks[:, pl.ds(256 * c, 256)]
        out = None
        for _ in range(3):
            part = x.astype(jnp.bfloat16)
            term = jnp.dot(p, part, preferred_element_type=jnp.float32)
            out = term if out is None else out + term
            x = x - part.astype(jnp.float32)
        send[c] = out


def dynamics(
    vol_ref, area_ref, vel_ref, forc_ref, cur_ref, strs_ref, mask_ref, own_ref,
    stress_out, vel_out,
    held, mask, own,
    f0, f1, f2, f3, f4, f5, f6, f7, f8,
    t0, t1, t2, t3, t4, t5, t6, t7, t8,
    g0, g1, g2, g3, g4, g5, g6, g7, g8,
    W, WE, WW, send_n, send_s, recv_s, recv_n,
    place, blocks, send,
    in_sem, halo_send, halo_recv, out_sem,
):
    F = (f0, f1, f2, f3, f4, f5, f6, f7, f8)
    T = (t0, t1, t2, t3, t4, t5, t6, t7, t8)
    G = (g0, g1, g2, g3, g4, g5, g6, g7, g8)
    gx, gy = lax.axis_index("gx"), lax.axis_index("gy")
    n_gx, n_gy = lax.axis_size("gx"), lax.axis_size("gy")
    east, west = lax.rem(gx + 1, n_gx), lax.rem(gx + n_gx - 1, n_gx)
    north, south = lax.rem(gy + 1, n_gy), lax.rem(gy + n_gy - 1, n_gy)

    has_e, has_w, has_n, has_s = gx < n_gx - 1, gx > 0, gy < n_gy - 1, gy > 0

    upper, lower = pl.ds(0, 64), pl.ds(64, 64)
    inner, mid = pl.ds(8, ROWS - 16), pl.ds(128, COLS - 256)
    left, right = pl.ds(0, 128), pl.ds(COLS - 128, 128)
    parts = (
        (upper, left),
        (upper, right),
        (lower, left),
        (lower, right),
        (pl.ds(0, 8), mid),
        (pl.ds(ROWS - 8, 8), mid),
        (inner, mid),
    )
    sources = (vol_ref, area_ref, vel_ref, forc_ref, cur_ref, strs_ref)

    def start_load(k):
        r, c = parts[k]
        start = 0
        for src in sources:
            dst = held.at[pl.ds(start, src.shape[0]), r, c]
            pltpu.make_async_copy(src.at[:, r, c], dst, in_sem.at[k]).start()
            start += src.shape[0]

    def wait_load(k):
        at = held.at[:, parts[k][0], parts[k][1]]
        pltpu.make_async_copy(at, at, in_sem.at[k]).wait()

    masks = [
        pltpu.make_async_copy(mask_ref.at[:, c], mask.at[:, c], in_sem.at[7 + k])
        for k, c in enumerate((left, right, mid))
    ]
    own_load = pltpu.make_async_copy(own_ref, own, in_sem.at[10])
    own_load.start()
    masks[0].start()
    masks[1].start()
    start_load(0)
    start_load(1)

    barrier = pltpu.get_barrier_semaphore()
    around = (
        (has_e, (east, gy)),
        (has_w, (west, gy)),
        (has_e & has_n, (east, north)),
        (has_e & has_s, (east, south)),
        (has_w & has_n, (west, north)),
        (has_w & has_s, (west, south)),
    )
    for there, device in around:

        @pl.when(there)
        def _(device=device):
            pl.semaphore_signal(barrier, inc=1, device_id=device, device_id_type=MESH)

    for k in range(1, 16):
        pl.semaphore_signal(
            barrier, inc=1, device_id=(gx, lax.rem(gy + k, n_gy)), device_id_type=MESH
        )
    one, zero = jnp.int32(1), jnp.int32(0)
    count = lambda there: jnp.where(there, one, zero)
    greeted = 15 + (count(has_e) + count(has_w)) * (1 + count(has_n) + count(has_s))

    start_load(2)
    start_load(3)
    start_load(4)
    start_load(5)
    masks[2].start()
    start_load(6)

    for buf, tiles, ends in ((F, 4, (8, 144)), (T, 4, (0, 32)), (G, 1, (0, 48))):
        for f in buf:
            for j in range(tiles):
                for r in ends:
                    f[j, pl.ds(r, 8), :] = jnp.zeros((8, 128), jnp.float32)
    above, below, same = pl.ds(TOP + ROWS, 8), pl.ds(TOP - 8, 8), pl.ds(TOP, ROWS)
    for there, buf in ((has_s, recv_s), (has_n, recv_n)):

        @pl.when(jnp.logical_not(there))
        def _(buf=buf):
            buf[...] = jnp.zeros(buf.shape, jnp.float32)

    for there, buf in ((has_e, WE), (has_w, WW)):
        for beside, at in ((has_n, above), (has_s, below), (there, same)):

            @pl.when(jnp.logical_not(there & beside))
            def _(buf=buf, at=at):
                buf[at, :] = jnp.zeros((at.size, 128), jnp.float32)

    first, last = W.at[pl.ds(0, 8), :], W.at[pl.ds(ROWS - 8, 8), :]
    halos = (
        (send_n, recv_s, (gx, north), has_n, has_s),
        (send_s, recv_n, (gx, south), has_s, has_n),
        (W, WW.at[same, :], (east, gy), has_e, has_w),
        (W, WE.at[same, :], (west, gy), has_w, has_e),
        (first, WW.at[above, :], (east, south), has_e & has_s, has_w & has_n),
        (first, WE.at[above, :], (west, south), has_w & has_s, has_e & has_n),
        (last, WW.at[below, :], (east, north), has_e & has_n, has_w & has_s),
        (last, WE.at[below, :], (west, north), has_w & has_n, has_e & has_s),
    )

    def halo(k):
        src, dst, device, _, _ = halos[k]
        return pltpu.make_async_remote_copy(
            src_ref=src,
            dst_ref=dst,
            send_sem=halo_send.at[k],
            recv_sem=halo_recv.at[k],
            device_id=device,
            device_id_type=MESH,
        )

    def start_halo(k):
        @pl.when(halos[k][3])
        def _():
            halo(k).start()

    own_load.wait()
    placing(own, place)

    masks[0].wait()
    masks[1].wait()
    for half in range(2):
        wait_load(2 * half)
        wait_load(2 * half + 1)
        prepare((held, mask), F, 64 * half, 1, 0, 64, (0, 3))
        pack_lon(F, W, 64 * half, 64)
    pl.semaphore_wait(barrier, greeted)
    for k in range(2, 8):
        start_halo(k)

    wait_load(4)
    wait_load(5)
    masks[2].wait()
    prepare((held, mask), F, 0, 2, ROWS - 8, 8, (1, 2))
    pack_lat(F, send_n, send_s)
    for k in (0, 1):
        start_halo(k)

    wait_load(6)
    prepare((held, mask), F, 8, 2, 56, 56, (1, 2))
    copy_edges(F, T, G)
    subcycles_inside(F)

    for k in range(8):

        @pl.when(halos[k][4])
        def _(k=k):
            halo(k).wait_recv()

    unpack_lat(T, G, recv_s, recv_n)
    unpack_lon(G, WE, WW)
    subcycles_edges(T, G)
    merge_edges(F, T, G, (U, V))
    flatten_blocks(F, blocks)
    gather_blocks(place, blocks, send)

    mine = pl.ds(pl.multiple_of(gy * 16, 16), 16)
    for to in OWNERS:

        @pl.when(gy != to)
        def _(to=to):
            pltpu.make_async_remote_copy(
                src_ref=send.at[:, pl.ds(pl.multiple_of(to * 16, 16), 16), :],
                dst_ref=vel_out.at[:, mine, :],
                send_sem=out_sem.at[0],
                recv_sem=out_sem.at[1],
                device_id=(gx, to),
                device_id_type=MESH,
            ).start()

    local = pltpu.make_async_copy(send.at[:, mine, :], vel_out.at[:, mine, :], out_sem.at[2])
    local.start()

    merge_edges(F, T, G, (N1, N2, SH))

    def rows(i, carry):
        src = pl.ds(pl.multiple_of(i * 16 + TOP, 8), 16)
        dst = pl.ds(pl.multiple_of(i * 16, 8), 16)
        for j in range(4):
            col = pl.ds(j * 128, 128)
            stress_out[0, dst, col] = 0.5 * (F[N1][j, src, :] + F[N2][j, src, :])
            stress_out[1, dst, col] = 0.5 * (F[N1][j, src, :] - F[N2][j, src, :])
            stress_out[2, dst, col] = 0.5 * F[SH][j, src, :]
        return carry

    lax.fori_loop(0, ROWS // 16, rows, 0)

    for k in range(8):

        @pl.when(halos[k][3])
        def _(k=k):
            halo(k).wait_send()

    others = pl.ds(0, 240)
    for k in range(2):
        pltpu.make_async_copy(send.at[:, others, :], vel_out.at[:, others, :], out_sem.at[k]).wait()
    local.wait()


def write_out(stress, vel, stress_out, vel_out, sem):
    copies = [
        pltpu.make_async_copy(stress, stress_out, sem.at[0]),
        pltpu.make_async_copy(vel, vel_out, sem.at[1]),
    ]
    for copy in copies:
        copy.start()
    for copy in copies:
        copy.wait()


def per_device(ice_volume, ice_area, velocity, forcing, current, stress, ice_mask, block_owner):
    f32, dma, vmem = jnp.float32, pltpu.SemaphoreType.DMA, pltpu.VMEM
    args = (ice_volume, ice_area, velocity, forcing, current, stress, ice_mask, block_owner)
    args = [pltpu.with_memory_space_constraint(a, pltpu.HBM) for a in args]
    stress_shape, vel_shape = (3, ROWS, COLS), (2, 256, 256)
    scratch = [vmem((19, ROWS, COLS), f32)] + [vmem(a.shape, a.dtype) for a in args[6:]]
    scratch += [vmem((4, HIGH, 128), f32)] * 9 + [vmem((4, 40, 128), f32)] * 9
    scratch += [vmem((1, 56, 128), f32)] * 9
    scratch += [vmem((ROWS, 128), f32), vmem((HIGH, 128), f32), vmem((HIGH, 128), f32)]
    scratch += [vmem((5, 4, 8, 128), f32)] * 4
    scratch += [vmem((256, 256), jnp.bfloat16), vmem((256, 512), f32), vmem(vel_shape, f32)]
    scratch += [dma((11,)), dma((8,)), dma((8,)), dma((3,))]
    held_stress, held_vel = pl.pallas_call(
        dynamics,
        out_shape=(vmem(stress_shape, f32), vmem(vel_shape, f32)),
        in_specs=[pl.BlockSpec(memory_space=pltpu.HBM)] * 8,
        out_specs=(pl.BlockSpec(memory_space=vmem),) * 2,
        scratch_shapes=scratch,
        compiler_params=pltpu.CompilerParams(
            collective_id=0, has_side_effects=True, vmem_limit_bytes=48 * 2**20
        ),
    )(*args)
    held_stress = pltpu.with_memory_space_constraint(held_stress, vmem)
    held_vel = pltpu.with_memory_space_constraint(held_vel, vmem)
    stress_out, vel_out = pl.pallas_call(
        write_out,
        out_shape=(
            jax.ShapeDtypeStruct(stress_shape, f32),
            jax.ShapeDtypeStruct(vel_shape, f32),
        ),
        in_specs=[pl.BlockSpec(memory_space=vmem)] * 2,
        out_specs=(pl.BlockSpec(memory_space=pl.ANY),) * 2,
        scratch_shapes=[dma((2,))],
    )(held_stress, held_vel)
    return (stress_out, vel_out[:, None])


def solution(mesh):
    tile = P(None, "gy", "gx")
    in_specs = (tile,) * 6 + (P("gy", "gx"),) * 2
    out_specs = (tile, P(None, "gx", "gy", None))
    return jax.shard_map(
        per_device, mesh=mesh, in_specs=in_specs, out_specs=out_specs, check_vma=False
    )
```
